32 devices in a mesh: grp: 2 (over y), space: 16 (over z, x, core).
Axes of the slice: x: 2, y: 2, z: 4, core: 2. Of those that a mesh axis runs over, the one named last changes fastest.
Arguments:
- snapshots: bfloat16 [2048, 3, 2048], P(('grp', 'space')), parts along dimension 0, may hold values from -6 to 6
- weights: float32 [4096], P(('grp', 'space')), parts along dimension 0, may hold values from 0.5 to 20, as said below
Outputs:
- spod_matrix: float32 [32, 30, 30], P('grp'), parts along dimension 0
The draws below stay inside these ranges and needn't reach their ends.
There are 2 independent parts, one for each index of `grp`. The reference program is written for one: setup_inputs(seed, part) draws one part's arguments, and reference() takes and returns one part's arrays. A program takes and returns all parts, laid end to end along the dimension named above; each array names one. Nothing has to cross between parts.
Inputs may be any that keep to these rules, and one draw needn't show every extreme that they name: Positive quadrature weights.
All inputs are finite; a program needn't handle non-finite values.
Results may differ from the reference program's by a relative error of at most 0.0003.
Values may be sent and summed in bfloat16 or wider, within the bound.
No kernel may reach another device: no remote copies, remote signals or barrier semaphores. Data moves between devices by JAX's collectives and lax.ppermute only.
A program may use at most 128 MiB of HBM per device.

```python
import math
import jax
import jax.numpy as jnp
from jax import lax

NFFT = 128
NB = 15
NF = 16
P_DEV = 128
NT = 1024
NPTS = 2048
N_SPACE = 16


def draw_weights(key, part):
    index = jnp.arange(NPTS, dtype=jnp.float32)
    ramp = jnp.exp(math.log(10.0) * index / NPTS)
    rough = jax.random.uniform(key, (NPTS,), jnp.float32, 0.5, 2.0)
    return (ramp * rough).astype(jnp.float32)


def levels(own_key, dims, cuts, low, largest):
    factor_of, own = 1.0, jax.random.fold_in(own_key, 6)
    for axis_at, shards_of in cuts:
        heights = jnp.exp(jax.random.uniform(jax.random.fold_in(own, axis_at), (shards_of,), jnp.float32, low / len(cuts), largest / len(cuts)))
        factor_of = factor_of * jnp.repeat(heights, dims[axis_at] // shards_of).reshape([-1 if axis == axis_at else 1 for axis in range(len(dims))])
    return factor_of


def bell_draw(own_key, dims, scale, reach, cuts=(), kind=jnp.bfloat16):
    factor_of = levels(own_key, dims, cuts, -0.22, 0.18) if cuts else 1.0
    entries = jax.random.normal(own_key, dims, jnp.float32) * scale * factor_of
    return jnp.minimum(jnp.maximum(entries, -reach), reach).astype(kind)


def setup_inputs(seed: int = 0, part: int = 0) -> dict:
    keys = jax.random.split(jax.random.key(seed), 3)
    part_splits = jax.random.split(jax.random.fold_in(keys[2], part), 3)
    return {
        "snapshots": bell_draw(part_splits[0], (NT, 3, NPTS), 1.0, 6.0, ((0, 16),)),
        "weights": draw_weights(jax.random.fold_in(jax.random.fold_in(keys[2], part), 71), part),
    }


def reference(snapshots, weights):
    half = NFFT // 2
    rows = 3 * P_DEV
    phase = jnp.arange(NFFT, dtype=jnp.float32)
    window = 0.5 - 0.5 * jnp.cos(2.0 * jnp.pi * phase / NFFT)
    norm = jnp.sqrt(jnp.sum(window * window))

    def slab_gram(carry, start):
        piece = lax.dynamic_slice_in_dim(snapshots, start, P_DEV, 2).astype(jnp.float32)
        weight_piece = lax.dynamic_slice_in_dim(weights, start, P_DEV, 0)
        signal = piece.reshape(NT, rows)
        signal = signal - lax.optimization_barrier(jnp.mean(signal, axis=0, keepdims=True))
        halves = signal.reshape(NB + 1, half, rows)
        blocks = jnp.concatenate([halves[:-1], halves[1:]], axis=1)
        blocks = blocks * (window / norm)[None, :, None]
        spectra = jnp.fft.fft(blocks, axis=1)[:, 1:NF + 1, :]
        columns = jnp.concatenate([jnp.real(spectra), jnp.imag(spectra)], axis=0)
        columns = jnp.transpose(columns, (1, 0, 2))
        row_weights = jnp.tile(weight_piece, 3)
        gram = jnp.einsum('fbr,fdr->fbd', columns * row_weights[None, None, :], columns, precision=lax.Precision.HIGHEST)
        return (carry + gram, None)
    starts = (jnp.arange(N_SPACE) * P_DEV).astype(jnp.int32)
    empty = jnp.zeros((NF, 2 * NB, 2 * NB), jnp.float32)
    summed, unused = lax.scan(slab_gram, empty, starts)
    return summed / jnp.sum(weights)
```

```python
import numpy as np
import ml_dtypes
import jax
import jax.numpy as jnp
from jax import lax
from jax.experimental import pallas as pl
from jax.experimental.pallas import tpu as pltpu
from jax.sharding import PartitionSpec as P

NFFT = 128
NB = 15
NF = 16
HALF = NFFT // 2
NH = NB + 1
LANES = 128
ROWS = 40
VMEM = 48 * 1024 * 1024


def half_table():
    turns = 2.0 * np.pi * np.arange(NF + 2)[:, None] * np.arange(HALF)[None, :] / NFFT
    re, im = np.cos(turns), -np.sin(turns)
    offset_re, offset_im = re.sum(1), im.sum(1)
    re0, im0 = re - re.mean(1, keepdims=True), im - im.mean(1, keepdims=True)
    table = np.zeros((ROWS, HALF))
    table[0:NF] = re0[1 : NF + 1]
    table[NF : 2 * NF] = im0[1 : NF + 1]
    table[32] = 1.0
    table[35] = re0[NF + 1]
    table[36] = im0[NF + 1]
    offsets = np.zeros((ROWS, 1))
    offsets[0:NF, 0] = offset_re[1 : NF + 1]
    offsets[NF : 2 * NF, 0] = offset_im[1 : NF + 1]
    offsets[35, 0] = offset_re[NF + 1]
    offsets[36, 0] = offset_im[NF + 1]
    return table, offsets.astype(np.float32)


def pieces(table, count):
    out, rest = [], table.astype(np.float64)
    for _ in range(count):
        part = rest.astype(np.float32).astype(ml_dtypes.bfloat16)
        out.append(part)
        rest = rest - part.astype(np.float64)
    return np.concatenate(out, axis=0)


def spectra_gram(halves, means, root, out_ref, tall_ref, offsets, steps_all):
    width = root.shape[1]
    total = means(0)
    for h in range(1, NH):
        total = total + means(h)
    mean = total * (1.0 / steps_all)
    freq = lax.broadcasted_iota(jnp.int32, (NF, 1), 0)
    sign = (2 * (freq & 1) - 1).astype(jnp.float32)
    lane = lax.broadcasted_iota(jnp.int32, (1, width), 1)
    held = None
    for h in range(NH):
        delta = means(h) * (1.0 / HALF) - mean
        rows = halves(h) + offsets * delta
        delta, rows = delta * root, rows * root
        re, im = rows[0:NF], rows[NF : 2 * NF]
        re_sides = jnp.concatenate([delta * float(HALF), re[:-1]], 0) + jnp.concatenate([re[1:], rows[35:36]], 0)
        im_sides = jnp.concatenate([jnp.zeros_like(delta), im[:-1]], 0) + jnp.concatenate([im[1:], rows[36:37]], 0)
        re2, im2 = re + re, im + im
        if h:
            tall_ref[h - 1, 0:NF] = held[0] + sign * (re2 + re_sides)
            tall_ref[h - 1, NF : 2 * NF] = held[1] + sign * (im2 + im_sides)
        held = (re2 - re_sides, im2 - im_sides)
    tall_ref[NH - 1, 0:NF] = jnp.broadcast_to(jnp.where(lane < LANES, root, 0.0), (NF, width))
    tall_ref[NH - 1, NF : 2 * NF] = jnp.zeros((NF, width), jnp.float32)
    tall = jnp.transpose(tall_ref[...], (1, 0, 2))
    group = NF // 2
    shared = lax.broadcasted_iota(jnp.int32, (NH, 4 * LANES // 2), 1) // NH % group
    dims = (((1,), (1,)), ((), ()))
    for g in range(2):
        part = [tall[i * NF + g * group : i * NF + (g + 1) * group].reshape(group * NH, width) for i in range(2)]
        rows = jnp.concatenate(part, 0)
        high = rows.astype(jnp.bfloat16)
        low = (rows - high.astype(jnp.float32)).astype(jnp.bfloat16)
        gram = lax.dot_general(high, high, dims, preferred_element_type=jnp.float32)
        gram = gram + lax.dot_general(high, low, dims, preferred_element_type=jnp.float32)
        gram = gram + lax.dot_general(low, high, dims, preferred_element_type=jnp.float32)
        gram = gram.reshape(2, group, NH, gram.shape[1])
        for i in range(2):
            kept = jnp.zeros(shared.shape, jnp.float32)
            for f in range(group):
                kept = kept + jnp.where(shared == f, gram[i, f], 0.0)
            out_ref[g, i] = kept


def gram_kernel(steps_all, block_ref, table_ref, offset_ref, weight_ref, out_ref, tall_ref, rows_ref):
    table = table_ref[...]
    for h in range(NH):
        block = jnp.concatenate([block_ref[h, c] for c in range(3)], axis=1)
        part = jnp.dot(table, block, preferred_element_type=jnp.float32)
        rows_ref[h] = part[0:ROWS] + part[ROWS : 2 * ROWS] + part[2 * ROWS :]
    root = jnp.sqrt(weight_ref[...])
    root = jnp.concatenate([root] * 3, axis=1)
    spectra_gram(
        lambda h: rows_ref[h], lambda h: rows_ref[h, 32:33, :], root, out_ref, tall_ref, offset_ref[...], steps_all
    )


def local_gram(block, weights, steps_all):
    table, offsets = half_table()
    width = block.shape[1] * block.shape[3]
    return pl.pallas_call(
        lambda *refs: gram_kernel(steps_all, *refs),
        out_shape=jax.ShapeDtypeStruct((2, 2, NH, 2 * LANES), jnp.float32),
        scratch_shapes=[
            pltpu.VMEM((NH, 2 * NF, width), jnp.float32),
            pltpu.VMEM((NH, ROWS, width), jnp.float32),
        ],
        compiler_params=pltpu.CompilerParams(vmem_limit_bytes=VMEM),
    )(block, jnp.asarray(pieces(table, 3)), jnp.asarray(offsets), weights[None, :])


def sum_over(value, axis, size):
    step = 1
    while step < size:
        value = value + lax.ppermute(value, axis, [(i, i ^ step) for i in range(size)])
        step *= 2
    return value


def unpack(summed):
    group = NF // 2
    whole = summed.reshape(2, 2, NH, 2, group, NH)
    weight_sum = whole[0, 0, NH - 1, 0, 0, NH - 1]
    whole = jnp.transpose(whole[:, :, :NB, :, :, :NB], (0, 4, 1, 2, 3, 5)).reshape(NF, 2 * NB, 2 * NB)
    return whole * (1.0 / (16.0 * 0.375 * NFFT)) / weight_sum


def make_local(n_space):
    def local(snapshots, weights):
        steps, components, points = snapshots.shape
        x = jnp.transpose(snapshots, (1, 0, 2)).reshape(components, steps, n_space, points // n_space)
        x = jnp.transpose(x, (2, 0, 1, 3))
        x = lax.all_to_all(x, "space", split_axis=0, concat_axis=0, tiled=True)
        steps_all = n_space * steps
        if steps != HALF:
            x = x.reshape(n_space * steps // HALF, HALF // steps, components, steps, -1)
            x = jnp.transpose(x, (0, 2, 1, 3, 4)).reshape(NH, components, HALF, -1)
        gram = local_gram(x, weights, steps_all)
        return unpack(sum_over(gram, "space", n_space))

    return local


def solution(mesh):
    in_specs = (P(("grp", "space"), None, None), P(("grp", "space")))
    out_specs = P("grp", None, None)
    return jax.shard_map(
        make_local(mesh.shape["space"]), mesh=mesh, in_specs=in_specs, out_specs=out_specs, check_vma=False
    )
```

```python
import numpy as np
import ml_dtypes
import jax
import jax.numpy as jnp
from jax import lax
from jax.experimental import pallas as pl
from jax.experimental.pallas import tpu as pltpu
from jax.sharding import PartitionSpec as P

NFFT = 128
NB = 15
NF = 16
HALF = NFFT // 2
NH = NB + 1
LANES = 128
MAIN = 2 * NF
EXTRA = 5
ROWS = 40
SMALLEST = 2.0**-60
VMEM = 48 * 1024 * 1024


def half_table():
    turns = 2.0 * np.pi * np.arange(NF + 2)[:, None] * np.arange(HALF)[None, :] / NFFT
    re, im = np.cos(turns), -np.sin(turns)
    offset_re, offset_im = re.sum(1), im.sum(1)
    re0, im0 = re - re.mean(1, keepdims=True), im - im.mean(1, keepdims=True)
    table = np.zeros((ROWS, HALF))
    table[0:NF] = re0[1 : NF + 1]
    table[NF : 2 * NF] = im0[1 : NF + 1]
    table[32] = 1.0
    table[35] = re0[NF + 1]
    table[36] = im0[NF + 1]
    offsets = np.zeros((ROWS, 1))
    offsets[0:NF, 0] = offset_re[1 : NF + 1]
    offsets[NF : 2 * NF, 0] = offset_im[1 : NF + 1]
    offsets[35, 0] = offset_re[NF + 1]
    offsets[36, 0] = offset_im[NF + 1]
    return table, offsets.astype(np.float32)


def pieces(table, count):
    out, rest = [], table.astype(np.float64)
    for _ in range(count):
        part = rest.astype(np.float32).astype(ml_dtypes.bfloat16)
        out.append(part)
        rest = rest - part.astype(np.float64)
    return np.concatenate(out, axis=0)


def transform_kernel(block_ref, table_ref, weight_ref, out_ref, root_ref):
    components, _, points = block_ref.shape
    table = table_ref[...]
    top = jnp.max(jnp.abs(block_ref[...].astype(jnp.float32)), axis=(0, 1, 2), keepdims=True)[0]
    power = jnp.floor(jnp.log2(jnp.maximum(top, SMALLEST)))
    scale = jnp.exp2(-power)
    extras = []
    for c in range(components):
        part = jnp.dot(table, block_ref[c], preferred_element_type=jnp.float32)
        rows = (part[0:ROWS] + part[ROWS : 2 * ROWS] + part[2 * ROWS :]) * scale
        for d in range(points // LANES):
            out_ref[d, c * MAIN : (c + 1) * MAIN] = rows[0:MAIN, d * LANES : (d + 1) * LANES]
        whole = rows[32:33]
        high = whole.astype(jnp.bfloat16).astype(jnp.float32)
        middle = (whole - high).astype(jnp.bfloat16).astype(jnp.float32)
        extras += [high, middle, whole - high - middle, rows[35:37]]
    extras.append(jnp.broadcast_to(power, (1, points)))
    extras = jnp.concatenate(extras, axis=0)
    for d in range(points // LANES):
        out_ref[d, components * MAIN :] = extras[:, d * LANES : (d + 1) * LANES]
    root_ref[...] = jnp.sqrt(weight_ref[...])


def gram_kernel(steps_all, rows_ref, offset_ref, root_ref, out_ref, tall_ref):
    components = (rows_ref.shape[1] - 1) // (MAIN + EXTRA)
    extra = components * MAIN

    def beside(h, at, step, count):
        return jnp.concatenate([rows_ref[h, at + c * step : at + c * step + count, :] for c in range(components)], 1)

    root = jnp.concatenate([root_ref[...]] * components, axis=1)
    offsets = offset_ref[...]
    sums, ends, scales, total = [], [], [], None
    for h in range(NH):
        further = beside(h, extra, EXTRA, EXTRA)
        power = rows_ref[h, extra + components * EXTRA : extra + components * EXTRA + 1, :]
        scale = jnp.concatenate([jnp.exp2(power)] * components, axis=1)
        sums.append((further[0:1] + further[1:2] + further[2:3]) * scale)
        ends.append(further[3:5])
        scales.append(scale)
        total = sums[0] if total is None else total + sums[h]
    mean = total * (1.0 / steps_all)
    freq = lax.broadcasted_iota(jnp.int32, (NF, 1), 0)
    sign = (2 * (freq & 1) - 1).astype(jnp.float32)
    lane = lax.broadcasted_iota(jnp.int32, root.shape, 1)
    held = None
    for h in range(NH):
        delta = (sums[h] * (1.0 / HALF) - mean) * root
        scale = scales[h] * root
        rows = beside(h, 0, MAIN, MAIN) * scale + offsets[0:MAIN] * delta
        end = ends[h] * scale + offsets[35:37] * delta
        re, im = rows[0:NF], rows[NF:MAIN]
        re_sides = jnp.concatenate([delta * float(HALF), re[:-1]], 0) + jnp.concatenate([re[1:], end[0:1]], 0)
        im_sides = jnp.concatenate([jnp.zeros_like(delta), im[:-1]], 0) + jnp.concatenate([im[1:], end[1:2]], 0)
        re2, im2 = re + re, im + im
        if h:
            tall_ref[h - 1, 0:NF] = held[0] + sign * (re2 + re_sides)
            tall_ref[h - 1, NF:MAIN] = held[1] + sign * (im2 + im_sides)
        held = (re2 - re_sides, im2 - im_sides)
    tall_ref[NH - 1, 0:NF] = jnp.broadcast_to(jnp.where(lane < LANES, root, 0.0), (NF, root.shape[1]))
    tall_ref[NH - 1, NF:MAIN] = jnp.zeros((NF, root.shape[1]), jnp.float32)
    tall = jnp.transpose(tall_ref[...], (1, 0, 2))
    group = NF // 2
    shared = lax.broadcasted_iota(jnp.int32, (NH, 2 * group * NH), 1) // NH % group
    dims = (((1,), (1,)), ((), ()))
    for g in range(2):
        part = [tall[i * NF + g * group : i * NF + (g + 1) * group].reshape(group * NH, -1) for i in range(2)]
        rows = jnp.concatenate(part, 0)
        high = rows.astype(jnp.bfloat16)
        low = (rows - high.astype(jnp.float32)).astype(jnp.bfloat16)
        gram = lax.dot_general(high, high, dims, preferred_element_type=jnp.float32)
        gram = gram + lax.dot_general(high, low, dims, preferred_element_type=jnp.float32)
        gram = gram + lax.dot_general(low, high, dims, preferred_element_type=jnp.float32)
        gram = gram.reshape(2, group, NH, gram.shape[1])
        for i in range(2):
            kept = jnp.zeros(shared.shape, jnp.float32)
            for f in range(group):
                kept = kept + jnp.where(shared == f, gram[i, f], 0.0)
            out_ref[g, i] = kept


def transform(block, weights):
    table, _ = half_table()
    components, _, points = block.shape
    return pl.pallas_call(
        transform_kernel,
        out_shape=(
            jax.ShapeDtypeStruct((points // LANES, components * (MAIN + EXTRA) + 1, LANES), jnp.float32),
            jax.ShapeDtypeStruct((1, LANES), jnp.float32),
        ),
        compiler_params=pltpu.CompilerParams(vmem_limit_bytes=VMEM),
    )(block, jnp.asarray(pieces(table, 3)), weights[None, :])


def local_gram(rows, root, steps_all):
    _, offsets = half_table()
    width = (rows.shape[1] - 1) // (MAIN + EXTRA) * LANES
    return pl.pallas_call(
        lambda *refs: gram_kernel(steps_all, *refs),
        out_shape=jax.ShapeDtypeStruct((2, 2, NH, 2 * LANES), jnp.float32),
        scratch_shapes=[pltpu.VMEM((NH, MAIN, width), jnp.float32)],
        compiler_params=pltpu.CompilerParams(vmem_limit_bytes=VMEM),
    )(rows, jnp.asarray(offsets), root)


def sum_over(value, axis, size):
    step = 1
    while step < size:
        value = value + lax.ppermute(value, axis, [(i, i ^ step) for i in range(size)])
        step *= 2
    return value


def unpack(summed):
    group = NF // 2
    whole = summed.reshape(2, 2, NH, 2, group, NH)
    weight_sum = whole[0, 0, NH - 1, 0, 0, NH - 1]
    whole = jnp.transpose(whole[:, :, :NB, :, :, :NB], (0, 4, 1, 2, 3, 5)).reshape(NF, 2 * NB, 2 * NB)
    return whole * (1.0 / (16.0 * 0.375 * NFFT)) / weight_sum


def make_local(n_space):
    def local(snapshots, weights):
        steps, components, points = snapshots.shape
        share = HALF // steps
        block = jnp.transpose(snapshots, (1, 0, 2))
        across = None
        if share > 1:
            block = block.reshape(components, steps, NH, share, -1)
            teams = [[h * share + i for i in range(share)] for h in range(NH)]
            block = lax.all_to_all(block, "space", split_axis=3, concat_axis=1, axis_index_groups=teams, tiled=True)
            block = block.reshape(components, HALF, -1)
            across = [[h * share + i for h in range(NH)] for i in range(share)]
        rows, root = transform(block, weights)
        rows = lax.all_to_all(
            rows.astype(jnp.float16), "space", split_axis=0, concat_axis=0, axis_index_groups=across, tiled=True
        )
        gram = local_gram(rows.astype(jnp.float32), root, n_space * steps)
        return unpack(sum_over(gram, "space", n_space))

    return local


def solution(mesh):
    in_specs = (P(("grp", "space"), None, None), P(("grp", "space")))
    out_specs = P("grp", None, None)
    return jax.shard_map(
        make_local(mesh.shape["space"]), mesh=mesh, in_specs=in_specs, out_specs=out_specs, check_vma=False
    )
```

```python
import numpy as np
import ml_dtypes
import jax
import jax.numpy as jnp
from jax import lax
from jax.experimental import pallas as pl
from jax.experimental.pallas import tpu as pltpu
from jax.sharding import PartitionSpec as P

NFFT = 128
NB = 15
NF = 16
HALF = NFFT // 2
NH = NB + 1
LANES = 128
MAIN = 2 * NF
EXTRA = 5
ROWS = 40
SMALLEST = 2.0**-60
VMEM = 48 * 1024 * 1024


def half_table():
    turns = 2.0 * np.pi * np.arange(NF + 2)[:, None] * np.arange(HALF)[None, :] / NFFT
    re, im = np.cos(turns), -np.sin(turns)
    offset_re, offset_im = re.sum(1), im.sum(1)
    re0, im0 = re - re.mean(1, keepdims=True), im - im.mean(1, keepdims=True)
    table = np.zeros((ROWS, HALF))
    table[0:NF] = re0[1 : NF + 1]
    table[NF : 2 * NF] = im0[1 : NF + 1]
    table[32] = 1.0
    table[35] = re0[NF + 1]
    table[36] = im0[NF + 1]
    offsets = np.zeros((ROWS, 1))
    offsets[0:NF, 0] = offset_re[1 : NF + 1]
    offsets[NF : 2 * NF, 0] = offset_im[1 : NF + 1]
    offsets[35, 0] = offset_re[NF + 1]
    offsets[36, 0] = offset_im[NF + 1]
    return table, offsets.astype(np.float32)


def pieces(table, count):
    out, rest = [], table.astype(np.float64)
    for _ in range(count):
        part = rest.astype(np.float32).astype(ml_dtypes.bfloat16)
        out.append(part)
        rest = rest - part.astype(np.float64)
    return np.concatenate(out, axis=0)


def transform_kernel(block_hbm, table_hbm, weight_hbm, offset_hbm, out_ref, root_ref, offset_ref, block_ref, table_ref, weight_ref, sems):
    components, _, points = block_ref.shape
    copies = [pltpu.make_async_copy(block_hbm.at[c], block_ref.at[c], sems.at[c]) for c in range(components)]
    copies.append(pltpu.make_async_copy(table_hbm, table_ref, sems.at[components]))
    copies.append(pltpu.make_async_copy(weight_hbm, weight_ref, sems.at[components + 1]))
    copies.append(pltpu.make_async_copy(offset_hbm, offset_ref, sems.at[components + 2]))
    for copy in copies:
        copy.start()
    for copy in copies:
        copy.wait()
    table = table_ref[...]
    top = jnp.max(jnp.abs(block_ref[...].astype(jnp.float32)), axis=(0, 1, 2), keepdims=True)[0]
    power = jnp.floor(jnp.log2(jnp.maximum(top, SMALLEST)))
    scale = jnp.exp2(-power)
    extras = []
    for c in range(components):
        part = jnp.dot(table, block_ref[c], preferred_element_type=jnp.float32)
        rows = (part[0:ROWS] + part[ROWS : 2 * ROWS] + part[2 * ROWS :]) * scale
        for d in range(points // LANES):
            out_ref[d, c * MAIN : (c + 1) * MAIN] = rows[0:MAIN, d * LANES : (d + 1) * LANES]
        whole = rows[32:33]
        high = whole.astype(jnp.bfloat16).astype(jnp.float32)
        middle = (whole - high).astype(jnp.bfloat16).astype(jnp.float32)
        extras += [high, middle, whole - high - middle, rows[35:37]]
    extras.append(jnp.broadcast_to(power, (1, points)))
    extras = jnp.concatenate(extras, axis=0)
    for d in range(points // LANES):
        out_ref[d, components * MAIN :] = extras[:, d * LANES : (d + 1) * LANES]
    root_ref[...] = jnp.sqrt(weight_ref[...])


def gram_kernel(steps_all, rows_ref, offset_ref, root_ref, out_ref, tall_ref):
    components = (rows_ref.shape[1] - 1) // (MAIN + EXTRA)
    extra = components * MAIN

    def beside(h, at, step, count):
        return jnp.concatenate([rows_ref[h, at + c * step : at + c * step + count, :] for c in range(components)], 1)

    root = jnp.concatenate([root_ref[...]] * components, axis=1)
    offsets = offset_ref[...]
    sums, ends, scales, total = [], [], [], None
    for h in range(NH):
        further = beside(h, extra, EXTRA, EXTRA)
        power = rows_ref[h, extra + components * EXTRA : extra + components * EXTRA + 1, :]
        scale = jnp.concatenate([jnp.exp2(power)] * components, axis=1)
        sums.append((further[0:1] + further[1:2] + further[2:3]) * scale)
        ends.append(further[3:5])
        scales.append(scale)
        total = sums[0] if total is None else total + sums[h]
    mean = total * (1.0 / steps_all)
    freq = lax.broadcasted_iota(jnp.int32, (NF, 1), 0)
    sign = (2 * (freq & 1) - 1).astype(jnp.float32)
    lane = lax.broadcasted_iota(jnp.int32, root.shape, 1)
    held = None
    for h in range(NH):
        delta = (sums[h] * (1.0 / HALF) - mean) * root
        scale = scales[h] * root
        rows = beside(h, 0, MAIN, MAIN) * scale + offsets[0:MAIN] * delta
        end = ends[h] * scale + offsets[35:37] * delta
        re, im = rows[0:NF], rows[NF:MAIN]
        re_sides = jnp.concatenate([delta * float(HALF), re[:-1]], 0) + jnp.concatenate([re[1:], end[0:1]], 0)
        im_sides = jnp.concatenate([jnp.zeros_like(delta), im[:-1]], 0) + jnp.concatenate([im[1:], end[1:2]], 0)
        re2, im2 = re + re, im + im
        if h:
            tall_ref[h - 1, 0:NF] = held[0] + sign * (re2 + re_sides)
            tall_ref[h - 1, NF:MAIN] = held[1] + sign * (im2 + im_sides)
        held = (re2 - re_sides, im2 - im_sides)
    tall_ref[NH - 1, 0:NF] = jnp.broadcast_to(jnp.where(lane < LANES, root, 0.0), (NF, root.shape[1]))
    tall_ref[NH - 1, NF:MAIN] = jnp.zeros((NF, root.shape[1]), jnp.float32)
    tall = jnp.transpose(tall_ref[...], (1, 0, 2))
    group = NF // 2
    shared = lax.broadcasted_iota(jnp.int32, (NH, 2 * group * NH), 1) // NH % group
    dims = (((1,), (1,)), ((), ()))
    for g in range(2):
        part = [tall[i * NF + g * group : i * NF + (g + 1) * group].reshape(group * NH, -1) for i in range(2)]
        rows = jnp.concatenate(part, 0)
        high = rows.astype(jnp.bfloat16)
        low = (rows - high.astype(jnp.float32)).astype(jnp.bfloat16)
        gram = lax.dot_general(high, high, dims, preferred_element_type=jnp.float32)
        gram = gram + lax.dot_general(high, low, dims, preferred_element_type=jnp.float32)
        gram = gram + lax.dot_general(low, high, dims, preferred_element_type=jnp.float32)
        gram = gram.reshape(2, group, NH, gram.shape[1])
        for i in range(2):
            kept = jnp.zeros(shared.shape, jnp.float32)
            for f in range(group):
                kept = kept + jnp.where(shared == f, gram[i, f], 0.0)
            out_ref[g, i] = kept


def transform(block, weights):
    table, offsets = half_table()
    components, _, points = block.shape
    table = pieces(table, 3)
    return pl.pallas_call(
        transform_kernel,
        in_specs=[pl.BlockSpec(memory_space=pltpu.HBM)] * 4,
        out_shape=(
            jax.ShapeDtypeStruct((points // LANES, components * (MAIN + EXTRA) + 1, LANES), jnp.float32),
            jax.ShapeDtypeStruct((1, LANES), jnp.float32),
            jax.ShapeDtypeStruct(offsets.shape, jnp.float32),
        ),
        scratch_shapes=[
            pltpu.VMEM(block.shape, block.dtype),
            pltpu.VMEM(table.shape, jnp.bfloat16),
            pltpu.VMEM((1, LANES), jnp.float32),
            pltpu.SemaphoreType.DMA((components + 3,)),
        ],
        compiler_params=pltpu.CompilerParams(vmem_limit_bytes=VMEM),
    )(block, jnp.asarray(table), weights[None, :], jnp.asarray(offsets))


def local_gram(rows, root, offsets, steps_all):
    width = (rows.shape[1] - 1) // (MAIN + EXTRA) * LANES
    return pl.pallas_call(
        lambda *refs: gram_kernel(steps_all, *refs),
        out_shape=jax.ShapeDtypeStruct((2, 2, NH, 2 * LANES), jnp.float32),
        scratch_shapes=[pltpu.VMEM((NH, MAIN, width), jnp.float32)],
        compiler_params=pltpu.CompilerParams(vmem_limit_bytes=VMEM),
    )(rows, offsets, root)


def partners(value, axis, size, steps):
    return [lax.ppermute(value, axis, [(i, i ^ step) for i in range(size)]) for step in steps]


def finish_kernel(*refs):
    out_ref = refs[-1]
    summed = refs[0][...]
    for ref in refs[1:-1]:
        summed = summed + ref[...]
    weight_sum = summed[0, 0, NB : NB + 1, NB : NB + 1]
    summed = summed * (1.0 / (16.0 * 0.375 * NFFT)) / weight_sum
    group = NF // 2
    squares = []
    for g in range(2):
        rows = summed[g].reshape(2 * NH, 2 * group * NH)
        for f in range(group):
            cuts = [rows[:, (i * group + f) * NH : (i * group + f) * NH + NB] for i in range(2)]
            squares.append(jnp.concatenate(cuts, axis=1))
    whole = jnp.transpose(jnp.stack(squares), (1, 0, 2))
    out_ref[0:NB] = whole[0:NB]
    out_ref[NB:] = whole[NH : NH + NB]


def finish(terms):
    out = pl.pallas_call(
        finish_kernel,
        out_shape=jax.ShapeDtypeStruct((2 * NB, NF, 2 * NB), jnp.float32),
        compiler_params=pltpu.CompilerParams(vmem_limit_bytes=VMEM),
    )(*terms)
    return jnp.transpose(out, (1, 0, 2))


def sum_over(value, axis, size):
    rounds, step = [], 1
    while step < size:
        wide = step == 2 and 4 * step <= size
        rounds.append([step, 2 * step, 3 * step] if wide else [step])
        step *= 4 if wide else 2
    for steps in rounds[:-1]:
        value = sum(partners(value, axis, size, steps), value)
    return [value] + partners(value, axis, size, rounds[-1])


def make_local(n_space):
    def local(snapshots, weights):
        steps, components, points = snapshots.shape
        share = HALF // steps
        block = jnp.transpose(snapshots, (1, 0, 2))
        across = None
        if share > 1:
            block = block.reshape(components, steps, NH, share, -1)
            teams = [[h * share + i for i in range(share)] for h in range(NH)]
            block = lax.all_to_all(block, "space", split_axis=3, concat_axis=1, axis_index_groups=teams, tiled=True)
            block = block.reshape(components, HALF, -1)
            across = [[h * share + i for h in range(NH)] for i in range(share)]
        rows, root, offsets = transform(block, weights)
        rows = lax.all_to_all(
            rows.astype(jnp.float16), "space", split_axis=0, concat_axis=0, axis_index_groups=across, tiled=True
        )
        gram = local_gram(rows.astype(jnp.float32), root, offsets, n_space * steps)
        return finish(sum_over(gram, "space", n_space))

    return local


def solution(mesh):
    in_specs = (P(("grp", "space"), None, None), P(("grp", "space")))
    out_specs = P("grp", None, None)
    return jax.shard_map(
        make_local(mesh.shape["space"]), mesh=mesh, in_specs=in_specs, out_specs=out_specs, check_vma=False
    )
```

```python
import numpy as np
import ml_dtypes
import jax
import jax.numpy as jnp
from jax import lax
from jax.experimental import pallas as pl
from jax.experimental.pallas import tpu as pltpu
from jax.sharding import PartitionSpec as P

NFFT = 128
NB = 15
NF = 16
HALF = NFFT // 2
NH = NB + 1
LANES = 128
MAIN = 2 * NF
EXTRA = 5
ROWS = 40
SMALLEST = 2.0**-60
VMEM = 48 * 1024 * 1024


def half_table():
    turns = 2.0 * np.pi * np.arange(NF + 2)[:, None] * np.arange(HALF)[None, :] / NFFT
    re, im = np.cos(turns), -np.sin(turns)
    offset_re, offset_im = re.sum(1), im.sum(1)
    re0, im0 = re - re.mean(1, keepdims=True), im - im.mean(1, keepdims=True)
    table = np.zeros((ROWS, HALF))
    table[0:NF] = re0[1 : NF + 1]
    table[NF : 2 * NF] = im0[1 : NF + 1]
    table[32] = 1.0
    table[35] = re0[NF + 1]
    table[36] = im0[NF + 1]
    offsets = np.zeros((ROWS, 1))
    offsets[0:NF, 0] = offset_re[1 : NF + 1]
    offsets[NF : 2 * NF, 0] = offset_im[1 : NF + 1]
    offsets[35, 0] = offset_re[NF + 1]
    offsets[36, 0] = offset_im[NF + 1]
    return table, offsets.astype(np.float32)


def pieces(table, count):
    out, rest = [], table.astype(np.float64)
    for _ in range(count):
        part = rest.astype(np.float32).astype(ml_dtypes.bfloat16)
        out.append(part)
        rest = rest - part.astype(np.float64)
    return np.concatenate(out, axis=0)


def transform_kernel(block_hbm, table_hbm, weight_hbm, offset_hbm, out_ref, root_ref, offset_ref, block_ref, table_ref, weight_ref, sems):
    components, _, points = block_ref.shape
    copies = [pltpu.make_async_copy(block_hbm.at[c], block_ref.at[c], sems.at[c]) for c in range(components)]
    copies.append(pltpu.make_async_copy(table_hbm, table_ref, sems.at[components]))
    copies.append(pltpu.make_async_copy(weight_hbm, weight_ref, sems.at[components + 1]))
    copies.append(pltpu.make_async_copy(offset_hbm, offset_ref, sems.at[components + 2]))
    for copy in copies:
        copy.start()
    for copy in copies:
        copy.wait()
    table = table_ref[...]
    top = jnp.max(jnp.abs(block_ref[...].astype(jnp.float32)), axis=(0, 1, 2), keepdims=True)[0]
    power = jnp.floor(jnp.log2(jnp.maximum(top, SMALLEST)))
    scale = jnp.exp2(-power)
    extras = []
    for c in range(components):
        part = jnp.dot(table, block_ref[c], preferred_element_type=jnp.float32)
        rows = (part[0:ROWS] + part[ROWS : 2 * ROWS] + part[2 * ROWS :]) * scale
        for d in range(points // LANES):
            out_ref[d, c * MAIN : (c + 1) * MAIN] = rows[0:MAIN, d * LANES : (d + 1) * LANES]
        whole = rows[32:33]
        high = whole.astype(jnp.bfloat16).astype(jnp.float32)
        middle = (whole - high).astype(jnp.bfloat16).astype(jnp.float32)
        extras += [high, middle, whole - high - middle, rows[35:37]]
    extras.append(jnp.broadcast_to(power, (1, points)))
    extras = jnp.concatenate(extras, axis=0)
    for d in range(points // LANES):
        out_ref[d, components * MAIN :] = extras[:, d * LANES : (d + 1) * LANES]
    root_ref[...] = jnp.sqrt(weight_ref[...])


def gram_kernel(steps_all, rows_ref, offset_ref, root_ref, out_ref, tall_ref):
    components = (rows_ref.shape[1] - 1) // (MAIN + EXTRA)
    extra = components * MAIN

    def beside(h, at, step, count):
        return jnp.concatenate([rows_ref[h, at + c * step : at + c * step + count, :] for c in range(components)], 1)

    root = jnp.concatenate([root_ref[...]] * components, axis=1)
    offsets = offset_ref[...]
    sums, ends, scales, total = [], [], [], None
    for h in range(NH):
        further = beside(h, extra, EXTRA, EXTRA)
        power = rows_ref[h, extra + components * EXTRA : extra + components * EXTRA + 1, :]
        scale = jnp.concatenate([jnp.exp2(power)] * components, axis=1)
        sums.append((further[0:1] + further[1:2] + further[2:3]) * scale)
        ends.append(further[3:5])
        scales.append(scale)
        total = sums[0] if total is None else total + sums[h]
    mean = total * (1.0 / steps_all)
    freq = lax.broadcasted_iota(jnp.int32, (NF, 1), 0)
    sign = (2 * (freq & 1) - 1).astype(jnp.float32)
    lane = lax.broadcasted_iota(jnp.int32, root.shape, 1)
    held = None
    for h in range(NH):
        delta = (sums[h] * (1.0 / HALF) - mean) * root
        scale = scales[h] * root
        rows = beside(h, 0, MAIN, MAIN) * scale + offsets[0:MAIN] * delta
        end = ends[h] * scale + offsets[35:37] * delta
        re, im = rows[0:NF], rows[NF:MAIN]
        re_sides = jnp.concatenate([delta * float(HALF), re[:-1]], 0) + jnp.concatenate([re[1:], end[0:1]], 0)
        im_sides = jnp.concatenate([jnp.zeros_like(delta), im[:-1]], 0) + jnp.concatenate([im[1:], end[1:2]], 0)
        re2, im2 = re + re, im + im
        if h:
            tall_ref[h - 1, 0:NF] = held[0] + sign * (re2 + re_sides)
            tall_ref[h - 1, NF:MAIN] = held[1] + sign * (im2 + im_sides)
        held = (re2 - re_sides, im2 - im_sides)
    tall_ref[NH - 1, 0:NF] = jnp.broadcast_to(jnp.where(lane < LANES, root, 0.0), (NF, root.shape[1]))
    tall_ref[NH - 1, NF:MAIN] = jnp.zeros((NF, root.shape[1]), jnp.float32)
    tall = jnp.transpose(tall_ref[...], (1, 0, 2))
    group = NF // 2
    row = lax.broadcasted_iota(jnp.int32, (NH, LANES), 0)
    column = lax.broadcasted_iota(jnp.int32, (NH, LANES), 1) % NH
    shared = lax.broadcasted_iota(jnp.int32, (NH, LANES), 1) // NH
    dims = (((1,), (1,)), ((), ()))
    for g in range(2):
        part = [tall[i * NF + g * group : i * NF + (g + 1) * group].reshape(group * NH, -1) for i in range(2)]
        rows = jnp.concatenate(part, 0)
        high = rows.astype(jnp.bfloat16)
        low = (rows - high.astype(jnp.float32)).astype(jnp.bfloat16)
        gram = lax.dot_general(high, high, dims, preferred_element_type=jnp.float32)
        gram = gram + lax.dot_general(high, low, dims, preferred_element_type=jnp.float32)
        gram = gram + lax.dot_general(low, high, dims, preferred_element_type=jnp.float32)
        gram = gram.reshape(2, group, NH, gram.shape[1])
        kept = []
        for i, j in ((0, 0), (1, 1), (0, 1)):
            block = jnp.zeros(shared.shape, jnp.float32)
            for f in range(group):
                block = block + jnp.where(shared == f, gram[i, f, :, j * LANES : (j + 1) * LANES], 0.0)
            kept.append(block)
        out_ref[g, :, 0:LANES] = jnp.where(column >= row, kept[0], jnp.concatenate([kept[0][0:1], kept[1][:-1]], 0))
        out_ref[g, :, LANES:] = kept[2]


def transform(block, weights):
    table, offsets = half_table()
    components, _, points = block.shape
    table = pieces(table, 3)
    return pl.pallas_call(
        transform_kernel,
        in_specs=[pl.BlockSpec(memory_space=pltpu.HBM)] * 4,
        out_shape=(
            jax.ShapeDtypeStruct((points // LANES, components * (MAIN + EXTRA) + 1, LANES), jnp.float32),
            jax.ShapeDtypeStruct((1, LANES), jnp.float32),
            jax.ShapeDtypeStruct(offsets.shape, jnp.float32),
        ),
        scratch_shapes=[
            pltpu.VMEM(block.shape, block.dtype),
            pltpu.VMEM(table.shape, jnp.bfloat16),
            pltpu.VMEM((1, LANES), jnp.float32),
            pltpu.SemaphoreType.DMA((components + 3,)),
        ],
        compiler_params=pltpu.CompilerParams(vmem_limit_bytes=VMEM),
    )(*[pltpu.with_memory_space_constraint(x, pltpu.HBM) for x in (block, jnp.asarray(table), weights[None, :], jnp.asarray(offsets))])


def local_gram(rows, root, offsets, steps_all):
    width = (rows.shape[1] - 1) // (MAIN + EXTRA) * LANES
    return pl.pallas_call(
        lambda *refs: gram_kernel(steps_all, *refs),
        out_shape=jax.ShapeDtypeStruct((2, NH, 2 * LANES), jnp.float32),
        scratch_shapes=[pltpu.VMEM((NH, MAIN, width), jnp.float32)],
        compiler_params=pltpu.CompilerParams(vmem_limit_bytes=VMEM),
    )(rows, offsets, root)


def partners(value, axis, size, steps):
    return [lax.ppermute(value, axis, [(i, i ^ step) for i in range(size)]) for step in steps]


def finish_kernel(*refs):
    out_ref = refs[-1]
    summed = refs[0][...]
    for ref in refs[1:-1]:
        summed = summed + ref[...]
    weight_sum = summed[0, NB : NB + 1, NB : NB + 1]
    summed = summed * (1.0 / (16.0 * 0.375 * NFFT)) / weight_sum
    cut, turned = [], []
    for which in range(2):
        half = summed[:, :, which * LANES : (which + 1) * LANES]
        cut.append(jnp.stack([half[g][:, f * NH : (f + 1) * NH] for g in range(2) for f in range(NF // 2)]))
        turned.append(jnp.concatenate([half[g].T.reshape(NF // 2, NH, NH) for g in range(2)], axis=0))
    row = lax.broadcasted_iota(jnp.int32, (NF, NB, NB), 1)
    column = lax.broadcasted_iota(jnp.int32, (NF, NB, NB), 2)
    re_re = jnp.where(row <= column, cut[0][:, 0:NB, 0:NB], turned[0][:, 0:NB, 0:NB])
    im_im = jnp.where(row >= column, cut[0][:, 1:NH, 0:NB], turned[0][:, 0:NB, 1:NH])
    upper = jnp.concatenate([re_re, cut[1][:, 0:NB, 0:NB]], axis=2)
    lower = jnp.concatenate([turned[1][:, 0:NB, 0:NB], im_im], axis=2)
    out_ref[0:NB] = jnp.transpose(upper, (1, 0, 2))
    out_ref[NB:] = jnp.transpose(lower, (1, 0, 2))


def finish(terms):
    out = pl.pallas_call(
        finish_kernel,
        out_shape=jax.ShapeDtypeStruct((2 * NB, NF, 2 * NB), jnp.float32),
        compiler_params=pltpu.CompilerParams(vmem_limit_bytes=VMEM),
    )(*terms)
    return jnp.transpose(out, (1, 0, 2))


def sum_over(value, axis, size):
    rounds, step = [], 1
    while step < size:
        wide = step == 2 and 4 * step <= size
        rounds.append([step, 2 * step, 3 * step] if wide else [step])
        step *= 4 if wide else 2
    for steps in rounds[:-1]:
        value = sum(partners(value, axis, size, steps), value)
    return [value] + partners(value, axis, size, rounds[-1])


def make_local(n_space):
    def local(snapshots, weights):
        steps, components, points = snapshots.shape
        share = HALF // steps
        block = jnp.transpose(snapshots, (1, 0, 2))
        across = None
        if share > 1:
            block = block.reshape(components, steps, NH, share, -1)
            teams = [[h * share + i for i in range(share)] for h in range(NH)]
            block = lax.all_to_all(block, "space", split_axis=3, concat_axis=1, axis_index_groups=teams, tiled=True)
            block = block.reshape(components, HALF, -1)
            across = [[h * share + i for h in range(NH)] for i in range(share)]
        rows, root, offsets = transform(block, weights)
        rows = lax.all_to_all(
            rows.astype(jnp.float16), "space", split_axis=0, concat_axis=0, axis_index_groups=across, tiled=True
        )
        gram = local_gram(rows.astype(jnp.float32), root, offsets, n_space * steps)
        return finish(sum_over(gram, "space", n_space))

    return local


def solution(mesh):
    in_specs = (P(("grp", "space"), None, None), P(("grp", "space")))
    out_specs = P("grp", None, None)
    return jax.shard_map(
        make_local(mesh.shape["space"]), mesh=mesh, in_specs=in_specs, out_specs=out_specs, check_vma=False
    )
```

```python
import numpy as np
import ml_dtypes
import jax
import jax.numpy as jnp
from jax import lax
from jax.experimental import pallas as pl
from jax.experimental.pallas import tpu as pltpu
from jax.sharding import PartitionSpec as P

NFFT = 128
NB = 15
NF = 16
HALF = NFFT // 2
NH = NB + 1
LANES = 128
MAIN = 2 * NF
EXTRA = 5
ROWS = 40
SMALLEST = 2.0**-60
VMEM = 48 * 1024 * 1024


def half_table():
    turns = 2.0 * np.pi * np.arange(NF + 2)[:, None] * np.arange(HALF)[None, :] / NFFT
    re, im = np.cos(turns), -np.sin(turns)
    offset_re, offset_im = re.sum(1), im.sum(1)
    re0, im0 = re - re.mean(1, keepdims=True), im - im.mean(1, keepdims=True)
    table = np.zeros((ROWS, HALF))
    table[0:NF] = re0[1 : NF + 1]
    table[NF : 2 * NF] = im0[1 : NF + 1]
    table[32] = 1.0
    table[35] = re0[NF + 1]
    table[36] = im0[NF + 1]
    offsets = np.zeros((ROWS, 1))
    offsets[0:NF, 0] = offset_re[1 : NF + 1]
    offsets[NF : 2 * NF, 0] = offset_im[1 : NF + 1]
    offsets[35, 0] = offset_re[NF + 1]
    offsets[36, 0] = offset_im[NF + 1]
    return table, offsets.astype(np.float32)


def pieces(table, count):
    out, rest = [], table.astype(np.float64)
    for _ in range(count):
        part = rest.astype(np.float32).astype(ml_dtypes.bfloat16)
        out.append(part)
        rest = rest - part.astype(np.float64)
    return np.concatenate(out, axis=0)


def transform_kernel(block_hbm, table_hbm, weight_hbm, offset_hbm, out_ref, root_ref, offset_ref, block_ref, table_ref, weight_ref, sems):
    components, _, points = block_ref.shape
    copies = [pltpu.make_async_copy(block_hbm.at[c], block_ref.at[c], sems.at[c]) for c in range(components)]
    copies.append(pltpu.make_async_copy(table_hbm, table_ref, sems.at[components]))
    copies.append(pltpu.make_async_copy(weight_hbm, weight_ref, sems.at[components + 1]))
    copies.append(pltpu.make_async_copy(offset_hbm, offset_ref, sems.at[components + 2]))
    for copy in copies:
        copy.start()
    for copy in copies:
        copy.wait()
    table = table_ref[...]
    top = jnp.max(jnp.abs(block_ref[...].astype(jnp.float32)), axis=(0, 1, 2), keepdims=True)[0]
    power = jnp.floor(jnp.log2(jnp.maximum(top, SMALLEST)))
    scale = jnp.exp2(-power)
    extras = []
    for c in range(components):
        part = jnp.dot(table, block_ref[c], preferred_element_type=jnp.float32)
        rows = (part[0:ROWS] + part[ROWS : 2 * ROWS] + part[2 * ROWS :]) * scale
        for d in range(points // LANES):
            out_ref[d, c * MAIN : (c + 1) * MAIN] = rows[0:MAIN, d * LANES : (d + 1) * LANES]
        whole = rows[32:33]
        high = whole.astype(jnp.bfloat16).astype(jnp.float32)
        middle = (whole - high).astype(jnp.bfloat16).astype(jnp.float32)
        extras += [high, middle, whole - high - middle, rows[35:37]]
    extras.append(jnp.broadcast_to(power, (1, points)))
    extras = jnp.concatenate(extras, axis=0)
    for d in range(points // LANES):
        out_ref[d, components * MAIN :] = extras[:, d * LANES : (d + 1) * LANES]
    root_ref[...] = jnp.sqrt(weight_ref[...])


def gram_kernel(steps_all, rows_ref, offset_ref, root_ref, out_ref, tall_ref):
    components = (rows_ref.shape[1] - 1) // (MAIN + EXTRA)
    extra = components * MAIN

    def beside(h, at, step, count):
        return jnp.concatenate([rows_ref[h, at + c * step : at + c * step + count, :] for c in range(components)], 1)

    root = jnp.concatenate([root_ref[...]] * components, axis=1)
    offsets = offset_ref[...]
    sums, ends, scales, total = [], [], [], None
    for h in range(NH):
        further = beside(h, extra, EXTRA, EXTRA)
        power = rows_ref[h, extra + components * EXTRA : extra + components * EXTRA + 1, :]
        scale = jnp.concatenate([jnp.exp2(power)] * components, axis=1)
        sums.append((further[0:1] + further[1:2] + further[2:3]) * scale)
        ends.append(further[3:5])
        scales.append(scale)
        total = sums[0] if total is None else total + sums[h]
    mean = total * (1.0 / steps_all)
    freq = lax.broadcasted_iota(jnp.int32, (NF, 1), 0)
    sign = (2 * (freq & 1) - 1).astype(jnp.float32)
    lane = lax.broadcasted_iota(jnp.int32, root.shape, 1)
    held = None
    for h in range(NH):
        delta = (sums[h] * (1.0 / HALF) - mean) * root
        scale = scales[h] * root
        rows = beside(h, 0, MAIN, MAIN) * scale + offsets[0:MAIN] * delta
        end = ends[h] * scale + offsets[35:37] * delta
        re, im = rows[0:NF], rows[NF:MAIN]
        re_sides = jnp.concatenate([delta * float(HALF), re[:-1]], 0) + jnp.concatenate([re[1:], end[0:1]], 0)
        im_sides = jnp.concatenate([jnp.zeros_like(delta), im[:-1]], 0) + jnp.concatenate([im[1:], end[1:2]], 0)
        re2, im2 = re + re, im + im
        if h:
            tall_ref[h - 1, 0:NF] = held[0] + sign * (re2 + re_sides)
            tall_ref[h - 1, NF:MAIN] = held[1] + sign * (im2 + im_sides)
        held = (re2 - re_sides, im2 - im_sides)
    tall_ref[NH - 1, 0:NF] = jnp.broadcast_to(jnp.where(lane < LANES, root, 0.0), (NF, root.shape[1]))
    tall_ref[NH - 1, NF:MAIN] = jnp.zeros((NF, root.shape[1]), jnp.float32)
    tall = jnp.transpose(tall_ref[...], (1, 0, 2))
    group = NF // 2
    row = lax.broadcasted_iota(jnp.int32, (NH, LANES), 0)
    column = lax.broadcasted_iota(jnp.int32, (NH, LANES), 1) % NH
    shared = lax.broadcasted_iota(jnp.int32, (NH, LANES), 1) // NH
    dims = (((1,), (1,)), ((), ()))
    for g in range(2):
        part = [tall[i * NF + g * group : i * NF + (g + 1) * group].reshape(group * NH, -1) for i in range(2)]
        rows = jnp.concatenate(part, 0)
        high = rows.astype(jnp.bfloat16)
        low = (rows - high.astype(jnp.float32)).astype(jnp.bfloat16)
        gram = lax.dot_general(high, high, dims, preferred_element_type=jnp.float32)
        gram = gram + lax.dot_general(high, low, dims, preferred_element_type=jnp.float32)
        gram = gram + lax.dot_general(low, high, dims, preferred_element_type=jnp.float32)
        gram = gram.reshape(2, group, NH, gram.shape[1])
        kept = []
        for i, j in ((0, 0), (1, 1), (0, 1)):
            block = jnp.zeros(shared.shape, jnp.float32)
            for f in range(group):
                block = block + jnp.where(shared == f, gram[i, f, :, j * LANES : (j + 1) * LANES], 0.0)
            kept.append(block)
        out_ref[g, :, 0:LANES] = jnp.where(column >= row, kept[0], jnp.concatenate([kept[0][0:1], kept[1][:-1]], 0))
        out_ref[g, :, LANES:] = kept[2]


def transform(block, weights):
    table, offsets = half_table()
    components, _, points = block.shape
    table = pieces(table, 3)
    return pl.pallas_call(
        transform_kernel,
        in_specs=[pl.BlockSpec(memory_space=pltpu.HBM)] * 4,
        out_shape=(
            jax.ShapeDtypeStruct((points // LANES, components * (MAIN + EXTRA) + 1, LANES), jnp.float32),
            jax.ShapeDtypeStruct((1, LANES), jnp.float32),
            jax.ShapeDtypeStruct(offsets.shape, jnp.float32),
        ),
        scratch_shapes=[
            pltpu.VMEM(block.shape, block.dtype),
            pltpu.VMEM(table.shape, jnp.bfloat16),
            pltpu.VMEM((1, LANES), jnp.float32),
            pltpu.SemaphoreType.DMA((components + 3,)),
        ],
        compiler_params=pltpu.CompilerParams(vmem_limit_bytes=VMEM),
    )(*[pltpu.with_memory_space_constraint(x, pltpu.HBM) for x in (block, jnp.asarray(table), weights[None, :], jnp.asarray(offsets))])


def local_gram(rows, root, offsets, steps_all):
    width = (rows.shape[1] - 1) // (MAIN + EXTRA) * LANES
    return pl.pallas_call(
        lambda *refs: gram_kernel(steps_all, *refs),
        out_shape=jax.ShapeDtypeStruct((2, NH, 2 * LANES), jnp.float32),
        scratch_shapes=[pltpu.VMEM((NH, MAIN, width), jnp.float32)],
        compiler_params=pltpu.CompilerParams(vmem_limit_bytes=VMEM),
    )(rows, offsets, root)


def partners(value, axis, size, steps):
    return [lax.ppermute(value, axis, [(i, i ^ step) for i in range(size)]) for step in steps]


def finish_kernel(*refs):
    out_ref = refs[-1]
    summed = refs[0][...]
    for ref in refs[1:-1]:
        summed = summed + ref[...]
    weight_sum = summed[0, NB : NB + 1, NB : NB + 1]
    summed = summed * (1.0 / (16.0 * 0.375 * NFFT)) / weight_sum
    cut, turned = [], []
    for which in range(2):
        half = summed[:, :, which * LANES : (which + 1) * LANES]
        cut.append(jnp.stack([half[g][:, f * NH : (f + 1) * NH] for g in range(2) for f in range(NF // 2)]))
        turned.append(jnp.concatenate([half[g].T.reshape(NF // 2, NH, NH) for g in range(2)], axis=0))
    row = lax.broadcasted_iota(jnp.int32, (NF, NB, NB), 1)
    column = lax.broadcasted_iota(jnp.int32, (NF, NB, NB), 2)
    re_re = jnp.where(row <= column, cut[0][:, 0:NB, 0:NB], turned[0][:, 0:NB, 0:NB])
    im_im = jnp.where(row >= column, cut[0][:, 1:NH, 0:NB], turned[0][:, 0:NB, 1:NH])
    upper = jnp.concatenate([re_re, cut[1][:, 0:NB, 0:NB]], axis=2)
    lower = jnp.concatenate([turned[1][:, 0:NB, 0:NB], im_im], axis=2)
    out_ref[0:NB] = jnp.transpose(upper, (1, 0, 2))
    out_ref[NB:] = jnp.transpose(lower, (1, 0, 2))


def finish(terms):
    out = pl.pallas_call(
        finish_kernel,
        out_shape=jax.ShapeDtypeStruct((2 * NB, NF, 2 * NB), jnp.float32),
        compiler_params=pltpu.CompilerParams(vmem_limit_bytes=VMEM),
    )(*terms)
    return jnp.transpose(out, (1, 0, 2))


def sum_over(value, axis, size):
    rounds, step = [], 1
    while step < size:
        wide = step == 2 and 4 * step <= size
        rounds.append([c + (step > 1) for c in ([step, 2 * step, 3 * step] if wide else [step])])
        step *= 4 if wide else 2
    for steps in rounds[:-1]:
        value = sum(partners(value, axis, size, steps), value)
    return [value] + partners(value, axis, size, rounds[-1])


def make_local(n_space):
    def local(snapshots, weights):
        steps, components, points = snapshots.shape
        share = HALF // steps
        block = jnp.transpose(snapshots, (1, 0, 2))
        across = None
        if share > 1:
            block = block.reshape(components, steps, NH, share, -1)
            teams = [[h * share + i for i in range(share)] for h in range(NH)]
            block = lax.all_to_all(block, "space", split_axis=3, concat_axis=1, axis_index_groups=teams, tiled=True)
            block = block.reshape(components, HALF, -1)
            across = [[h * share + i for h in range(NH)] for i in range(share)]
        rows, root, offsets = transform(block, weights)
        rows = lax.all_to_all(
            rows.astype(jnp.float16), "space", split_axis=0, concat_axis=0, axis_index_groups=across, tiled=True
        )
        gram = local_gram(rows.astype(jnp.float32), root, offsets, n_space * steps)
        return finish(sum_over(gram, "space", n_space))

    return local


def solution(mesh):
    in_specs = (P(("grp", "space"), None, None), P(("grp", "space")))
    out_specs = P("grp", None, None)
    return jax.shard_map(
        make_local(mesh.shape["space"]), mesh=mesh, in_specs=in_specs, out_specs=out_specs, check_vma=False
    )
```

```python
import numpy as np
import ml_dtypes
import jax
import jax.numpy as jnp
from jax import lax
from jax.experimental import pallas as pl
from jax.experimental.pallas import tpu as pltpu
from jax.sharding import PartitionSpec as P

NFFT = 128
NB = 15
NF = 16
HALF = NFFT // 2
NH = NB + 1
LANES = 128
MAIN = 2 * NF
EXTRA = 5
ROWS = 40
SMALLEST = 2.0**-60
VMEM = 48 * 1024 * 1024


def half_table():
    turns = 2.0 * np.pi * np.arange(NF + 2)[:, None] * np.arange(HALF)[None, :] / NFFT
    re, im = np.cos(turns), -np.sin(turns)
    offset_re, offset_im = re.sum(1), im.sum(1)
    re0, im0 = re - re.mean(1, keepdims=True), im - im.mean(1, keepdims=True)
    table = np.zeros((ROWS, HALF))
    table[0:NF] = re0[1 : NF + 1]
    table[NF : 2 * NF] = im0[1 : NF + 1]
    table[32] = 1.0
    table[35] = re0[NF + 1]
    table[36] = im0[NF + 1]
    offsets = np.zeros((ROWS, 1))
    offsets[0:NF, 0] = offset_re[1 : NF + 1]
    offsets[NF : 2 * NF, 0] = offset_im[1 : NF + 1]
    offsets[35, 0] = offset_re[NF + 1]
    offsets[36, 0] = offset_im[NF + 1]
    return table, offsets.astype(np.float32)


def pieces(table):
    high = table.astype(ml_dtypes.bfloat16)
    low = (table - high.astype(np.float64)).astype(ml_dtypes.bfloat16)
    for row in range(table.shape[0]):
        for _ in range(8):
            left = table[row].sum() - high[row].astype(np.float64).sum() - low[row].astype(np.float64).sum()
            moved = (low[row].astype(np.float64) + left).astype(ml_dtypes.bfloat16)
            error = np.abs(moved.astype(np.float64) - low[row].astype(np.float64) - left)
            at = int(np.argmin(error))
            if error[at] >= abs(left):
                break
            low[row, at] = moved[at]
    return np.concatenate([high, low], axis=1)


def transform_kernel(block_hbm, table_hbm, weight_hbm, offset_hbm, out_ref, root_ref, offset_ref, block_ref, table_ref, weight_ref, sems):
    components, _, points = block_ref.shape
    copies = [pltpu.make_async_copy(block_hbm.at[c], block_ref.at[c], sems.at[c]) for c in range(components)]
    copies.append(pltpu.make_async_copy(table_hbm, table_ref, sems.at[components]))
    copies.append(pltpu.make_async_copy(weight_hbm, weight_ref, sems.at[components + 1]))
    copies.append(pltpu.make_async_copy(offset_hbm, offset_ref, sems.at[components + 2]))
    for copy in copies:
        copy.start()
    for copy in copies:
        copy.wait()
    table = table_ref[...]
    top = jnp.max(jnp.abs(block_ref[...].astype(jnp.float32)), axis=(0, 1, 2), keepdims=True)[0]
    power = jnp.floor(jnp.log2(jnp.maximum(top, SMALLEST)))
    scale = jnp.exp2(-power)
    extras = []
    for c in range(components):
        block = block_ref[c]
        rows = jnp.dot(table, jnp.concatenate([block] * 2, axis=0), preferred_element_type=jnp.float32) * scale
        for d in range(points // LANES):
            out_ref[d, c * MAIN : (c + 1) * MAIN] = rows[0:MAIN, d * LANES : (d + 1) * LANES]
        whole = rows[32:33]
        high = whole.astype(jnp.bfloat16).astype(jnp.float32)
        middle = (whole - high).astype(jnp.bfloat16).astype(jnp.float32)
        extras += [high, middle, whole - high - middle, rows[35:37]]
    extras.append(jnp.broadcast_to(power, (1, points)))
    extras = jnp.concatenate(extras, axis=0)
    for d in range(points // LANES):
        out_ref[d, components * MAIN :] = extras[:, d * LANES : (d + 1) * LANES]
    root_ref[...] = jnp.sqrt(weight_ref[...])


def gram_kernel(steps_all, rows_ref, offset_ref, root_ref, out_ref, tall_ref):
    components = (rows_ref.shape[1] - 1) // (MAIN + EXTRA)
    extra = components * MAIN

    def beside(h, at, step, count):
        return jnp.concatenate([rows_ref[h, at + c * step : at + c * step + count, :] for c in range(components)], 1)

    root = jnp.concatenate([root_ref[...]] * components, axis=1)
    offsets = offset_ref[...]
    sums, ends, scales, total = [], [], [], None
    for h in range(NH):
        further = beside(h, extra, EXTRA, EXTRA)
        power = rows_ref[h, extra + components * EXTRA : extra + components * EXTRA + 1, :]
        scale = jnp.concatenate([jnp.exp2(power)] * components, axis=1)
        sums.append((further[0:1] + further[1:2] + further[2:3]) * scale)
        ends.append(further[3:5])
        scales.append(scale)
        total = sums[0] if total is None else total + sums[h]
    mean = total * (1.0 / steps_all)
    freq = lax.broadcasted_iota(jnp.int32, (NF, 1), 0)
    sign = (2 * (freq & 1) - 1).astype(jnp.float32)
    lane = lax.broadcasted_iota(jnp.int32, root.shape, 1)
    held = None
    for h in range(NH):
        delta = (sums[h] * (1.0 / HALF) - mean) * root
        scale = scales[h] * root
        rows = beside(h, 0, MAIN, MAIN) * scale + offsets[0:MAIN] * delta
        end = ends[h] * scale + offsets[35:37] * delta
        re, im = rows[0:NF], rows[NF:MAIN]
        re_sides = jnp.concatenate([delta * float(HALF), re[:-1]], 0) + jnp.concatenate([re[1:], end[0:1]], 0)
        im_sides = jnp.concatenate([jnp.zeros_like(delta), im[:-1]], 0) + jnp.concatenate([im[1:], end[1:2]], 0)
        re2, im2 = re + re, im + im
        if h:
            tall_ref[h - 1, 0:NF] = held[0] + sign * (re2 + re_sides)
            tall_ref[h - 1, NF:MAIN] = held[1] + sign * (im2 + im_sides)
        held = (re2 - re_sides, im2 - im_sides)
    tall_ref[NH - 1, 0:NF] = jnp.broadcast_to(jnp.where(lane < LANES, root, 0.0), (NF, root.shape[1]))
    tall_ref[NH - 1, NF:MAIN] = jnp.zeros((NF, root.shape[1]), jnp.float32)
    tall = jnp.transpose(tall_ref[...], (1, 0, 2))
    group = NF // 2
    row = lax.broadcasted_iota(jnp.int32, (NH, LANES), 0)
    column = lax.broadcasted_iota(jnp.int32, (NH, LANES), 1) % NH
    shared = lax.broadcasted_iota(jnp.int32, (NH, LANES), 1) // NH
    dims = (((1,), (1,)), ((), ()))
    for g in range(2):
        part = [tall[i * NF + g * group : i * NF + (g + 1) * group].reshape(group * NH, -1) for i in range(2)]
        rows = jnp.concatenate(part, 0)
        high = rows.astype(jnp.bfloat16)
        low = (rows - high.astype(jnp.float32)).astype(jnp.bfloat16)
        left, right = jnp.concatenate([high, high, low], 1), jnp.concatenate([high, low, high], 1)
        gram = lax.dot_general(left, right, dims, preferred_element_type=jnp.float32)
        gram = gram.reshape(2, group, NH, gram.shape[1])
        kept = []
        for i, j in ((0, 0), (1, 1), (0, 1)):
            block = jnp.zeros(shared.shape, jnp.float32)
            for f in range(group):
                block = block + jnp.where(shared == f, gram[i, f, :, j * LANES : (j + 1) * LANES], 0.0)
            kept.append(block)
        out_ref[g, :, 0:LANES] = jnp.where(column >= row, kept[0], jnp.concatenate([kept[0][0:1], kept[1][:-1]], 0))
        out_ref[g, :, LANES:] = kept[2]


def transform(block, weights):
    table, offsets = half_table()
    components, _, points = block.shape
    table = pieces(table)
    return pl.pallas_call(
        transform_kernel,
        in_specs=[pl.BlockSpec(memory_space=pltpu.HBM)] * 4,
        out_shape=(
            jax.ShapeDtypeStruct((points // LANES, components * (MAIN + EXTRA) + 1, LANES), jnp.float32),
            jax.ShapeDtypeStruct((1, LANES), jnp.float32),
            jax.ShapeDtypeStruct(offsets.shape, jnp.float32),
        ),
        scratch_shapes=[
            pltpu.VMEM(block.shape, block.dtype),
            pltpu.VMEM(table.shape, jnp.bfloat16),
            pltpu.VMEM((1, LANES), jnp.float32),
            pltpu.SemaphoreType.DMA((components + 3,)),
        ],
        compiler_params=pltpu.CompilerParams(vmem_limit_bytes=VMEM),
    )(*[pltpu.with_memory_space_constraint(x, pltpu.HBM) for x in (block, jnp.asarray(table), weights[None, :], jnp.asarray(offsets))])


def local_gram(rows, root, offsets, steps_all):
    width = (rows.shape[1] - 1) // (MAIN + EXTRA) * LANES
    return pl.pallas_call(
        lambda *refs: gram_kernel(steps_all, *refs),
        out_shape=jax.ShapeDtypeStruct((2, NH, 2 * LANES), jnp.float32),
        scratch_shapes=[pltpu.VMEM((NH, MAIN, width), jnp.float32)],
        compiler_params=pltpu.CompilerParams(vmem_limit_bytes=VMEM),
    )(rows, offsets, root)


def partners(value, axis, size, steps):
    return [lax.ppermute(value, axis, [(i, i ^ step) for i in range(size)]) for step in steps]


def finish_kernel(*refs):
    out_ref = refs[-1]
    summed = refs[0][...]
    for ref in refs[1:-1]:
        summed = summed + ref[...]
    weight_sum = summed[0, NB : NB + 1, NB : NB + 1]
    summed = summed * (1.0 / (16.0 * 0.375 * NFFT)) / weight_sum
    cut, turned = [], []
    for which in range(2):
        half = summed[:, :, which * LANES : (which + 1) * LANES]
        cut.append(jnp.stack([half[g][:, f * NH : (f + 1) * NH] for g in range(2) for f in range(NF // 2)]))
        turned.append(jnp.concatenate([half[g].T.reshape(NF // 2, NH, NH) for g in range(2)], axis=0))
    row = lax.broadcasted_iota(jnp.int32, (NF, NB, NB), 1)
    column = lax.broadcasted_iota(jnp.int32, (NF, NB, NB), 2)
    re_re = jnp.where(row <= column, cut[0][:, 0:NB, 0:NB], turned[0][:, 0:NB, 0:NB])
    im_im = jnp.where(row >= column, cut[0][:, 1:NH, 0:NB], turned[0][:, 0:NB, 1:NH])
    upper = jnp.concatenate([re_re, cut[1][:, 0:NB, 0:NB]], axis=2)
    lower = jnp.concatenate([turned[1][:, 0:NB, 0:NB], im_im], axis=2)
    out_ref[0:NB] = jnp.transpose(upper, (1, 0, 2))
    out_ref[NB:] = jnp.transpose(lower, (1, 0, 2))


def finish(terms):
    out = pl.pallas_call(
        finish_kernel,
        out_shape=jax.ShapeDtypeStruct((2 * NB, NF, 2 * NB), jnp.float32),
        compiler_params=pltpu.CompilerParams(vmem_limit_bytes=VMEM),
    )(*terms)
    return jnp.transpose(out, (1, 0, 2))


def sum_over(value, axis, size):
    rounds, step = [], 1
    while step < size:
        wide = step == 2 and 4 * step <= size
        rounds.append([c + (step > 1) for c in ([step, 2 * step, 3 * step] if wide else [step])])
        step *= 4 if wide else 2
    for steps in rounds[:-1]:
        value = sum(partners(value, axis, size, steps), value)
    return [value] + partners(value, axis, size, rounds[-1])


def make_local(n_space):
    def local(snapshots, weights):
        steps, components, points = snapshots.shape
        share = HALF // steps
        block = jnp.transpose(snapshots, (1, 0, 2))
        across = None
        if share > 1:
            block = block.reshape(components, steps, NH, share, -1)
            teams = [[h * share + i for i in range(share)] for h in range(NH)]
            block = lax.all_to_all(block, "space", split_axis=3, concat_axis=1, axis_index_groups=teams, tiled=True)
            block = block.reshape(components, HALF, -1)
            across = [[h * share + i for h in range(NH)] for i in range(share)]
        rows, root, offsets = transform(block, weights)
        rows = lax.all_to_all(
            rows.astype(jnp.float16), "space", split_axis=0, concat_axis=0, axis_index_groups=across, tiled=True
        )
        gram = local_gram(rows.astype(jnp.float32), root, offsets, n_space * steps)
        return finish(sum_over(gram, "space", n_space))

    return local


def solution(mesh):
    in_specs = (P(("grp", "space"), None, None), P(("grp", "space")))
    out_specs = P("grp", None, None)
    return jax.shard_map(
        make_local(mesh.shape["space"]), mesh=mesh, in_specs=in_specs, out_specs=out_specs, check_vma=False
    )
```

```python
import numpy as np
import ml_dtypes
import jax
import jax.numpy as jnp
from jax import lax
from jax.experimental import pallas as pl
from jax.experimental.pallas import tpu as pltpu
from jax.sharding import PartitionSpec as P

NFFT = 128
NB = 15
NF = 16
HALF = NFFT // 2
NH = NB + 1
LANES = 128
MAIN = 2 * NF
EXTRA = 5
ROWS = 40
SMALLEST = 2.0**-60
SMALL_SUM = 1024.0
LOWEST, STEEP = -14.0, 29.9
VMEM = 48 * 1024 * 1024


def half_table():
    turns = 2.0 * np.pi * np.arange(NF + 2)[:, None] * np.arange(HALF)[None, :] / NFFT
    re, im = np.cos(turns), -np.sin(turns)
    offset_re, offset_im = re.sum(1), im.sum(1)
    re0, im0 = re - re.mean(1, keepdims=True), im - im.mean(1, keepdims=True)
    table = np.zeros((ROWS, HALF))
    table[0:NF] = re0[1 : NF + 1]
    table[NF : 2 * NF] = im0[1 : NF + 1]
    table[32] = 1.0 / SMALL_SUM
    table[35] = re0[NF + 1]
    table[36] = im0[NF + 1]
    return table, (offset_re.tolist(), offset_im.tolist())


def pieces(table):
    high = table.astype(ml_dtypes.bfloat16)
    low = (table - high.astype(np.float64)).astype(ml_dtypes.bfloat16)
    for row in range(table.shape[0]):
        for _ in range(8):
            left = table[row].sum() - high[row].astype(np.float64).sum() - low[row].astype(np.float64).sum()
            moved = (low[row].astype(np.float64) + left).astype(ml_dtypes.bfloat16)
            error = np.abs(moved.astype(np.float64) - low[row].astype(np.float64) - left)
            at = int(np.argmin(error))
            if error[at] >= abs(left):
                break
            low[row, at] = moved[at]
    return np.concatenate([high, low], axis=1)


def spread(component):
    place = lax.broadcasted_iota(jnp.int32, (1, LANES), 1) + LANES * component
    turns = place.astype(jnp.float32) * 0.618034
    return 1.0 / (1.0 + 0.125 * (turns - jnp.floor(turns)))


def transform_kernel(block_hbm, table_hbm, weight_hbm, out_ref, root_ref, block_ref, table_ref, weight_ref, sems):
    components, _, points = block_ref.shape
    copies = [pltpu.make_async_copy(block_hbm.at[c], block_ref.at[c], sems.at[c]) for c in range(components)]
    copies.append(pltpu.make_async_copy(table_hbm, table_ref, sems.at[components]))
    copies.append(pltpu.make_async_copy(weight_hbm, weight_ref, sems.at[components + 1]))
    for copy in copies:
        copy.start()
    for copy in copies:
        copy.wait()
    table = table_ref[...]
    extras = []
    for c in range(components):
        block = block_ref[c]
        rows = jnp.dot(table, jnp.concatenate([block] * 2, axis=0), preferred_element_type=jnp.float32)
        sizes = jnp.abs(rows)
        top = sizes[:, 0:LANES]
        for d in range(1, points // LANES):
            top = jnp.maximum(top, sizes[:, d * LANES : (d + 1) * LANES])
        eighths = jnp.ceil(8.0 * jnp.log2(jnp.maximum(jnp.max(top, axis=0, keepdims=True), SMALLEST)))
        scale = jnp.exp2(eighths * -0.125) * spread(c)
        scale, eighths = (jnp.concatenate([x] * (points // LANES), axis=1) for x in (scale, eighths))
        coded = jnp.exp2(sizes * (scale * STEEP) + LOWEST)
        coded = jnp.where(rows < 0.0, -coded, coded)
        for d in range(points // LANES):
            out_ref[d, c * MAIN : (c + 1) * MAIN] = coded[0:MAIN, d * LANES : (d + 1) * LANES]
        whole = rows[32:33] * (scale * SMALL_SUM)
        shifted = whole * 8193.0
        high = shifted - (shifted - whole)
        extras += [high, whole - high, coded[35:37], eighths]
    extras.append(jnp.zeros((1, points), jnp.float32))
    extras = jnp.concatenate(extras, axis=0)
    for d in range(points // LANES):
        out_ref[d, components * MAIN :] = extras[:, d * LANES : (d + 1) * LANES]
    root_ref[...] = jnp.sqrt(weight_ref[...])


def gram_kernel(steps_all, offsets, rows_ref, root_ref, out_ref, high_ref, low_ref):
    components = (rows_ref.shape[1] - 1) // (MAIN + EXTRA)
    extra = components * MAIN
    group = NF // 2
    rows = jnp.transpose(rows_ref[...], (1, 0, 2))
    root = root_ref[...]
    last = lax.broadcasted_iota(jnp.int32, (NH, LANES), 0) == NB
    for c in range(components):
        further = rows[extra + c * EXTRA : extra + (c + 1) * EXTRA]
        scale = jnp.exp2(further[4] * 0.125) * (1.0 / spread(c))
        sums = (further[0] + further[1]) * scale
        delta = (sums * (1.0 / HALF) - jnp.sum(sums, axis=0, keepdims=True) * (1.0 / steps_all)) * root
        scale = scale * (root * (1.0 / STEEP))

        def value(i, k):
            coded = rows[c * MAIN + i * NF + k - 1] if k <= NF else further[2 + i]
            size = (jnp.log2(jnp.abs(coded)) - LOWEST) * scale
            return jnp.where(coded < 0.0, -size, size) + (offsets[i][k] * delta if k % 2 else 0.0)

        for i in range(2):
            before, here = (delta * float(HALF), jnp.zeros_like(delta))[i], value(i, 1)
            for k in range(1, NF + 1):
                after = value(i, k + 1)
                sides, twice = before + after, here + here
                back = pltpu.roll(twice + sides, NH - 1, 0)
                spectrum = twice - sides - back if k % 2 else twice - sides + back
                spectrum = jnp.where(last, root if i == 0 and c == 0 else 0.0, spectrum)
                high = spectrum.astype(jnp.bfloat16)
                g, f = (k - 1) // group, (k - 1) % group
                at = pl.ds((i * group + f) * NH, NH)
                high_ref[g, at, c * LANES : (c + 1) * LANES] = high
                low_ref[g, at, c * LANES : (c + 1) * LANES] = (spectrum - high.astype(jnp.float32)).astype(jnp.bfloat16)
                before, here = here, after
    row = lax.broadcasted_iota(jnp.int32, (NH, LANES), 0)
    column = lax.broadcasted_iota(jnp.int32, (NH, LANES), 1) % NH
    shared = lax.broadcasted_iota(jnp.int32, (NH, LANES), 1) // NH
    dims = (((1,), (1,)), ((), ()))
    for g in range(2):
        high, low = high_ref[g], low_ref[g]
        left, right = jnp.concatenate([high, high, low], 1), jnp.concatenate([high, low, high], 1)
        gram = lax.dot_general(left, right, dims, preferred_element_type=jnp.float32)
        gram = gram.reshape(2, group, NH, gram.shape[1])
        kept = []
        for i, j in ((0, 0), (1, 1), (0, 1)):
            block = jnp.zeros(shared.shape, jnp.float32)
            for f in range(group):
                block = block + jnp.where(shared == f, gram[i, f, :, j * LANES : (j + 1) * LANES], 0.0)
            kept.append(block)
        out_ref[g, :, 0:LANES] = jnp.where(column >= row, kept[0], jnp.concatenate([kept[0][0:1], kept[1][:-1]], 0))
        out_ref[g, :, LANES:] = kept[2]


def transform(block, weights):
    table, _ = half_table()
    components, _, points = block.shape
    table = pieces(table)
    return pl.pallas_call(
        transform_kernel,
        in_specs=[pl.BlockSpec(memory_space=pltpu.HBM)] * 3,
        out_shape=(
            jax.ShapeDtypeStruct((points // LANES, components * (MAIN + EXTRA) + 1, LANES), jnp.float32),
            jax.ShapeDtypeStruct((1, LANES), jnp.float32),
        ),
        scratch_shapes=[
            pltpu.VMEM(block.shape, block.dtype),
            pltpu.VMEM(table.shape, jnp.bfloat16),
            pltpu.VMEM((1, LANES), jnp.float32),
            pltpu.SemaphoreType.DMA((components + 2,)),
        ],
        compiler_params=pltpu.CompilerParams(vmem_limit_bytes=VMEM),
    )(*[pltpu.with_memory_space_constraint(x, pltpu.HBM) for x in (block, jnp.asarray(table), weights[None, :])])


def local_gram(rows, root, steps_all):
    _, offsets = half_table()
    width = (rows.shape[1] - 1) // (MAIN + EXTRA) * LANES
    return pl.pallas_call(
        lambda *refs: gram_kernel(steps_all, offsets, *refs),
        out_shape=jax.ShapeDtypeStruct((2, NH, 2 * LANES), jnp.float32),
        scratch_shapes=[pltpu.VMEM((2, NF * NH, width), jnp.bfloat16)] * 2,
        compiler_params=pltpu.CompilerParams(vmem_limit_bytes=VMEM),
    )(rows, root)


def partners(value, axis, size, steps):
    return [lax.ppermute(value, axis, [(i, i ^ step) for i in range(size)]) for step in steps]


def finish_kernel(*refs):
    out_ref = refs[-1]
    summed = refs[0][...]
    for ref in refs[1:-1]:
        summed = summed + ref[...]
    weight_sum = summed[0, NB : NB + 1, NB : NB + 1]
    summed = summed * (1.0 / (16.0 * 0.375 * NFFT)) / weight_sum
    cut, turned = [], []
    for which in range(2):
        half = summed[:, :, which * LANES : (which + 1) * LANES]
        cut.append(jnp.stack([half[g][:, f * NH : (f + 1) * NH] for g in range(2) for f in range(NF // 2)]))
        turned.append(jnp.concatenate([half[g].T.reshape(NF // 2, NH, NH) for g in range(2)], axis=0))
    row = lax.broadcasted_iota(jnp.int32, (NF, NB, NB), 1)
    column = lax.broadcasted_iota(jnp.int32, (NF, NB, NB), 2)
    re_re = jnp.where(row <= column, cut[0][:, 0:NB, 0:NB], turned[0][:, 0:NB, 0:NB])
    im_im = jnp.where(row >= column, cut[0][:, 1:NH, 0:NB], turned[0][:, 0:NB, 1:NH])
    upper = jnp.concatenate([re_re, cut[1][:, 0:NB, 0:NB]], axis=2)
    lower = jnp.concatenate([turned[1][:, 0:NB, 0:NB], im_im], axis=2)
    out_ref[0:NB] = jnp.transpose(upper, (1, 0, 2))
    out_ref[NB:] = jnp.transpose(lower, (1, 0, 2))


def finish(terms):
    out = pl.pallas_call(
        finish_kernel,
        out_shape=jax.ShapeDtypeStruct((2 * NB, NF, 2 * NB), jnp.float32),
        compiler_params=pltpu.CompilerParams(vmem_limit_bytes=VMEM),
    )(*terms)
    return jnp.transpose(out, (1, 0, 2))


def sum_over(value, axis, size):
    rounds, step = [], 1
    while step < size:
        wide = step == 2 and 4 * step <= size
        rounds.append([c + (step > 1) for c in ([step, 2 * step, 3 * step] if wide else [step])])
        step *= 4 if wide else 2
    for steps in rounds[:-1]:
        value = sum(partners(value, axis, size, steps), value)
    return [value] + partners(value, axis, size, rounds[-1])


def make_local(n_space):
    def local(snapshots, weights):
        steps, components, points = snapshots.shape
        share = HALF // steps
        block = jnp.transpose(snapshots, (1, 0, 2))
        across = None
        if share > 1:
            block = block.reshape(components, steps, NH, share, -1)
            teams = [[h * share + i for i in range(share)] for h in range(NH)]
            block = lax.all_to_all(block, "space", split_axis=3, concat_axis=1, axis_index_groups=teams, tiled=True)
            block = block.reshape(components, HALF, -1)
            across = [[h * share + i for h in range(NH)] for i in range(share)]
        rows, root = transform(block, weights)
        rows = lax.all_to_all(
            rows.astype(jnp.float16), "space", split_axis=0, concat_axis=0, axis_index_groups=across, tiled=True
        )
        gram = local_gram(rows.astype(jnp.float32), root, n_space * steps)
        return finish(sum_over(gram, "space", n_space))

    return local


def solution(mesh):
    in_specs = (P(("grp", "space"), None, None), P(("grp", "space")))
    out_specs = P("grp", None, None)
    return jax.shard_map(
        make_local(mesh.shape["space"]), mesh=mesh, in_specs=in_specs, out_specs=out_specs, check_vma=False
    )
```

```python
import numpy as np
import ml_dtypes
import jax
import jax.numpy as jnp
from jax import lax
from jax.experimental import pallas as pl
from jax.experimental.pallas import tpu as pltpu
from jax.sharding import PartitionSpec as P

NFFT = 128
NB = 15
NF = 16
HALF = NFFT // 2
NH = NB + 1
LANES = 128
MAIN = 2 * NF
EXTRA = 5
ROWS = 40
SMALLEST = 2.0**-60
SMALL_SUM = 256.0
LOWEST, STEEP = -125.0, 251.0
VMEM = 48 * 1024 * 1024


def half_table():
    turns = 2.0 * np.pi * np.arange(NF + 2)[:, None] * np.arange(HALF)[None, :] / NFFT
    re, im = np.cos(turns), -np.sin(turns)
    offset_re, offset_im = re.sum(1), im.sum(1)
    re0, im0 = re - re.mean(1, keepdims=True), im - im.mean(1, keepdims=True)
    table = np.zeros((ROWS, HALF))
    table[0:NF] = re0[1 : NF + 1]
    table[NF : 2 * NF] = im0[1 : NF + 1]
    table[32] = 1.0 / SMALL_SUM
    table[35] = re0[NF + 1]
    table[36] = im0[NF + 1]
    return table, (offset_re.tolist(), offset_im.tolist())


def pieces(table):
    high = table.astype(ml_dtypes.bfloat16)
    low = (table - high.astype(np.float64)).astype(ml_dtypes.bfloat16)
    for row in range(table.shape[0]):
        for _ in range(8):
            left = table[row].sum() - high[row].astype(np.float64).sum() - low[row].astype(np.float64).sum()
            moved = (low[row].astype(np.float64) + left).astype(ml_dtypes.bfloat16)
            error = np.abs(moved.astype(np.float64) - low[row].astype(np.float64) - left)
            at = int(np.argmin(error))
            if error[at] >= abs(left):
                break
            low[row, at] = moved[at]
    return np.concatenate([high, low], axis=1)


def spread(component):
    place = lax.broadcasted_iota(jnp.int32, (1, LANES), 1) + LANES * component
    turns = place.astype(jnp.float32) * 0.618034
    return 1.0 / (1.0 + 0.125 * (turns - jnp.floor(turns)))


def coded_of(values, sizes, scale):
    coded = jnp.exp2(sizes * (scale * STEEP) + LOWEST)
    return jnp.where(values < 0.0, -coded, coded)


def value_of(coded, scale):
    size = (jnp.log2(jnp.abs(coded)) - LOWEST) * scale
    return jnp.where(coded < 0.0, -size, size)


def transform_kernel(block_hbm, table_hbm, weight_hbm, out_ref, root_ref, block_ref, table_ref, weight_ref, sems):
    components, _, points = block_ref.shape
    copies = [pltpu.make_async_copy(block_hbm.at[c], block_ref.at[c], sems.at[c]) for c in range(components)]
    copies.append(pltpu.make_async_copy(table_hbm, table_ref, sems.at[components]))
    copies.append(pltpu.make_async_copy(weight_hbm, weight_ref, sems.at[components + 1]))
    for copy in copies:
        copy.start()
    for copy in copies:
        copy.wait()
    table = table_ref[...]
    extras = []
    for c in range(components):
        block = block_ref[c]
        rows = jnp.dot(table, jnp.concatenate([block] * 2, axis=0), preferred_element_type=jnp.float32)
        sizes = jnp.abs(rows)
        top = sizes[:, 0:LANES]
        for d in range(1, points // LANES):
            top = jnp.maximum(top, sizes[:, d * LANES : (d + 1) * LANES])
        halves = jnp.ceil(2.0 * jnp.log2(jnp.maximum(jnp.max(top, axis=0, keepdims=True), SMALLEST)))
        scale = jnp.exp2(halves * -0.5) * spread(c)
        scale, halves = (jnp.concatenate([x] * (points // LANES), axis=1) for x in (scale, halves))
        coded = coded_of(rows, sizes, scale)
        for d in range(points // LANES):
            out_ref[d, c * MAIN : (c + 1) * MAIN] = coded[0:MAIN, d * LANES : (d + 1) * LANES].astype(jnp.bfloat16)
        whole = rows[32:33] * SMALL_SUM
        high = whole.astype(jnp.bfloat16).astype(jnp.float32)
        rest = whole - high
        extras += [high, coded_of(rest, jnp.abs(rest), scale), coded[35:37], halves]
    extras.append(jnp.zeros((1, points), jnp.float32))
    extras = jnp.concatenate(extras, axis=0).astype(jnp.bfloat16)
    for d in range(points // LANES):
        out_ref[d, components * MAIN :] = extras[:, d * LANES : (d + 1) * LANES]
    root_ref[...] = jnp.sqrt(weight_ref[...])


def gram_kernel(steps_all, offsets, rows_ref, root_ref, out_ref, high_ref, low_ref):
    components = (rows_ref.shape[1] - 1) // (MAIN + EXTRA)
    extra = components * MAIN
    group = NF // 2
    rows = jnp.transpose(rows_ref[...].astype(jnp.float32), (1, 0, 2))
    root = root_ref[...]
    last = lax.broadcasted_iota(jnp.int32, (NH, LANES), 0) == NB
    for c in range(components):
        further = rows[extra + c * EXTRA : extra + (c + 1) * EXTRA]
        scale = jnp.exp2(further[4] * 0.5) * (1.0 / (STEEP * spread(c)))
        sums = further[0] + value_of(further[1], scale)
        delta = (sums * (1.0 / HALF) - jnp.sum(sums, axis=0, keepdims=True) * (1.0 / steps_all)) * root
        scale = scale * root

        def value(i, k):
            coded = rows[c * MAIN + i * NF + k - 1] if k <= NF else further[2 + i]
            return value_of(coded, scale) + (offsets[i][k] * delta if k % 2 else 0.0)

        for i in range(2):
            before, here = (delta * float(HALF), jnp.zeros_like(delta))[i], value(i, 1)
            for k in range(1, NF + 1):
                after = value(i, k + 1)
                sides, twice = before + after, here + here
                back = pltpu.roll(twice + sides, NH - 1, 0)
                spectrum = twice - sides - back if k % 2 else twice - sides + back
                spectrum = jnp.where(last, root if i == 0 and c == 0 else 0.0, spectrum)
                high = spectrum.astype(jnp.bfloat16)
                g, f = (k - 1) // group, (k - 1) % group
                at = pl.ds((i * group + f) * NH, NH)
                high_ref[g, at, c * LANES : (c + 1) * LANES] = high
                low_ref[g, at, c * LANES : (c + 1) * LANES] = (spectrum - high.astype(jnp.float32)).astype(jnp.bfloat16)
                before, here = here, after
    row = lax.broadcasted_iota(jnp.int32, (NH, LANES), 0)
    column = lax.broadcasted_iota(jnp.int32, (NH, LANES), 1) % NH
    shared = lax.broadcasted_iota(jnp.int32, (NH, LANES), 1) // NH
    dims = (((1,), (1,)), ((), ()))
    for g in range(2):
        high, low = high_ref[g], low_ref[g]
        left, right = jnp.concatenate([high, high, low], 1), jnp.concatenate([high, low, high], 1)
        gram = lax.dot_general(left, right, dims, preferred_element_type=jnp.float32)
        gram = gram.reshape(2, group, NH, gram.shape[1])
        kept = []
        for i, j in ((0, 0), (1, 1), (0, 1)):
            block = jnp.zeros(shared.shape, jnp.float32)
            for f in range(group):
                block = block + jnp.where(shared == f, gram[i, f, :, j * LANES : (j + 1) * LANES], 0.0)
            kept.append(block)
        out_ref[g, :, 0:LANES] = jnp.where(column >= row, kept[0], jnp.concatenate([kept[0][0:1], kept[1][:-1]], 0))
        out_ref[g, :, LANES:] = kept[2]


def transform(block, weights):
    table, _ = half_table()
    components, _, points = block.shape
    table = pieces(table)
    return pl.pallas_call(
        transform_kernel,
        in_specs=[pl.BlockSpec(memory_space=pltpu.HBM)] * 3,
        out_shape=(
            jax.ShapeDtypeStruct((points // LANES, components * (MAIN + EXTRA) + 1, LANES), jnp.bfloat16),
            jax.ShapeDtypeStruct((1, LANES), jnp.float32),
        ),
        scratch_shapes=[
            pltpu.VMEM(block.shape, block.dtype),
            pltpu.VMEM(table.shape, jnp.bfloat16),
            pltpu.VMEM((1, LANES), jnp.float32),
            pltpu.SemaphoreType.DMA((components + 2,)),
        ],
        compiler_params=pltpu.CompilerParams(vmem_limit_bytes=VMEM),
    )(*[pltpu.with_memory_space_constraint(x, pltpu.HBM) for x in (block, jnp.asarray(table), weights[None, :])])


def local_gram(rows, root, steps_all):
    _, offsets = half_table()
    width = (rows.shape[1] - 1) // (MAIN + EXTRA) * LANES
    return pl.pallas_call(
        lambda *refs: gram_kernel(steps_all, offsets, *refs),
        out_shape=jax.ShapeDtypeStruct((2, NH, 2 * LANES), jnp.float32),
        scratch_shapes=[pltpu.VMEM((2, NF * NH, width), jnp.bfloat16)] * 2,
        compiler_params=pltpu.CompilerParams(vmem_limit_bytes=VMEM),
    )(rows, root)


def partners(value, axis, size, steps):
    return [lax.ppermute(value, axis, [(i, i ^ step) for i in range(size)]) for step in steps]


def finish_kernel(*refs):
    out_ref = refs[-1]
    summed = refs[0][...]
    for ref in refs[1:-1]:
        summed = summed + ref[...]
    weight_sum = summed[0, NB : NB + 1, NB : NB + 1]
    summed = summed * (1.0 / (16.0 * 0.375 * NFFT)) / weight_sum
    cut, turned = [], []
    for which in range(2):
        half = summed[:, :, which * LANES : (which + 1) * LANES]
        cut.append(jnp.stack([half[g][:, f * NH : (f + 1) * NH] for g in range(2) for f in range(NF // 2)]))
        turned.append(jnp.concatenate([half[g].T.reshape(NF // 2, NH, NH) for g in range(2)], axis=0))
    row = lax.broadcasted_iota(jnp.int32, (NF, NB, NB), 1)
    column = lax.broadcasted_iota(jnp.int32, (NF, NB, NB), 2)
    re_re = jnp.where(row <= column, cut[0][:, 0:NB, 0:NB], turned[0][:, 0:NB, 0:NB])
    im_im = jnp.where(row >= column, cut[0][:, 1:NH, 0:NB], turned[0][:, 0:NB, 1:NH])
    upper = jnp.concatenate([re_re, cut[1][:, 0:NB, 0:NB]], axis=2)
    lower = jnp.concatenate([turned[1][:, 0:NB, 0:NB], im_im], axis=2)
    out_ref[0:NB] = jnp.transpose(upper, (1, 0, 2))
    out_ref[NB:] = jnp.transpose(lower, (1, 0, 2))


def finish(terms):
    out = pl.pallas_call(
        finish_kernel,
        out_shape=jax.ShapeDtypeStruct((2 * NB, NF, 2 * NB), jnp.float32),
        compiler_params=pltpu.CompilerParams(vmem_limit_bytes=VMEM),
    )(*terms)
    return jnp.transpose(out, (1, 0, 2))


def sum_over(value, axis, size):
    rounds, step = [], 1
    while step < size:
        wide = step == 2 and 4 * step <= size
        rounds.append([c + (step > 1) for c in ([step, 2 * step, 3 * step] if wide else [step])])
        step *= 4 if wide else 2
    for steps in rounds[:-1]:
        value = sum(partners(value, axis, size, steps), value)
    return [value] + partners(value, axis, size, rounds[-1])


def make_local(n_space):
    def local(snapshots, weights):
        steps, components, points = snapshots.shape
        share = HALF // steps
        block = jnp.transpose(snapshots, (1, 0, 2))
        across = None
        if share > 1:
            block = block.reshape(components, steps, NH, share, -1)
            teams = [[h * share + i for i in range(share)] for h in range(NH)]
            block = lax.all_to_all(block, "space", split_axis=3, concat_axis=1, axis_index_groups=teams, tiled=True)
            block = block.reshape(components, HALF, -1)
            across = [[h * share + i for h in range(NH)] for i in range(share)]
        rows, root = transform(block, weights)
        rows = lax.all_to_all(rows, "space", split_axis=0, concat_axis=0, axis_index_groups=across, tiled=True)
        gram = local_gram(rows, root, n_space * steps)
        return finish(sum_over(gram, "space", n_space))

    return local


def solution(mesh):
    in_specs = (P(("grp", "space"), None, None), P(("grp", "space")))
    out_specs = P("grp", None, None)
    return jax.shard_map(
        make_local(mesh.shape["space"]), mesh=mesh, in_specs=in_specs, out_specs=out_specs, check_vma=False
    )
```

```python
import math

import numpy as np
import ml_dtypes
import jax
import jax.numpy as jnp
from jax import lax
from jax.experimental import pallas as pl
from jax.experimental.pallas import tpu as pltpu
from jax.sharding import PartitionSpec as P

NFFT = 128
NB = 15
NF = 16
HALF = NFFT // 2
NH = NB + 1
LANES = 128
MAIN = 2 * NF
EXTRA = 5
ROWS = 40
SMALLEST = 2.0**-60
SMALL_SUM = 256.0
LOWEST, STEEP = -125.0, 251.0
VMEM = 48 * 1024 * 1024


def half_table():
    turns = 2.0 * np.pi * np.arange(NF + 2)[:, None] * np.arange(HALF)[None, :] / NFFT
    re, im = np.cos(turns), -np.sin(turns)
    offset_re, offset_im = re.sum(1), im.sum(1)
    re0, im0 = re - re.mean(1, keepdims=True), im - im.mean(1, keepdims=True)
    table = np.zeros((ROWS, HALF))
    table[0:NF] = re0[1 : NF + 1]
    table[NF : 2 * NF] = im0[1 : NF + 1]
    table[32] = 1.0 / SMALL_SUM
    table[35] = re0[NF + 1]
    table[36] = im0[NF + 1]
    return table, (offset_re.tolist(), offset_im.tolist())


def pieces(table):
    high = table.astype(ml_dtypes.bfloat16)
    low = (table - high.astype(np.float64)).astype(ml_dtypes.bfloat16)
    for row in range(table.shape[0]):
        for _ in range(8):
            left = table[row].sum() - high[row].astype(np.float64).sum() - low[row].astype(np.float64).sum()
            moved = (low[row].astype(np.float64) + left).astype(ml_dtypes.bfloat16)
            error = np.abs(moved.astype(np.float64) - low[row].astype(np.float64) - left)
            at = int(np.argmin(error))
            if error[at] >= abs(left):
                break
            low[row, at] = moved[at]
    return np.concatenate([high, low], axis=1)


def spread(component):
    place = lax.broadcasted_iota(jnp.int32, (1, LANES), 1) + LANES * component
    turns = place.astype(jnp.float32) * 0.618034
    return 1.0 / (1.0 + 0.125 * (turns - jnp.floor(turns)))


def coded_of(values, sizes, scale):
    coded = jnp.exp2(sizes * (scale * STEEP) + LOWEST)
    return jnp.where(values < 0.0, -coded, coded)


def value_of(coded, scale):
    return (jnp.log2(jnp.abs(coded)) - LOWEST) * jnp.where(coded < 0.0, -scale, scale)


def transform_kernel(block_hbm, table_hbm, weight_hbm, out_ref, root_ref, block_ref, table_ref, weight_ref, sems):
    components, _, points = block_ref.shape
    copies = [pltpu.make_async_copy(block_hbm.at[c], block_ref.at[c], sems.at[c]) for c in range(components)]
    copies.append(pltpu.make_async_copy(table_hbm, table_ref, sems.at[components]))
    copies.append(pltpu.make_async_copy(weight_hbm, weight_ref, sems.at[components + 1]))
    for copy in copies:
        copy.start()
    for copy in copies:
        copy.wait()
    table = table_ref[...]
    place = lax.broadcasted_iota(jnp.int32, (8, 1), 0)
    many = math.gcd(points // LANES, 4)
    wide = many * LANES
    for p in range(points // wide):
        extras = []
        for c in range(components):
            block = block_ref[c, :, p * wide : (p + 1) * wide]
            rows = jnp.dot(table, jnp.concatenate([block] * 2, axis=0), preferred_element_type=jnp.float32)
            sizes = jnp.abs(rows)
            top = sizes[:, 0:LANES]
            for d in range(1, many):
                top = jnp.maximum(top, sizes[:, d * LANES : (d + 1) * LANES])
            halves = jnp.ceil(2.0 * jnp.log2(jnp.maximum(jnp.max(top, axis=0, keepdims=True), SMALLEST)))
            scale = jnp.exp2(halves * -0.5) * spread(c)
            scale, halves = (jnp.concatenate([x] * many, axis=1) for x in (scale, halves))
            whole = rows[32:33] * SMALL_SUM
            high = whole.astype(jnp.bfloat16).astype(jnp.float32)
            rows = jnp.concatenate([rows[0:32], jnp.where(place == 1, whole - high, rows[32:40])], axis=0)
            coded = coded_of(rows, jnp.abs(rows), scale)
            for d in range(many):
                out_ref[p * many + d, c * MAIN : (c + 1) * MAIN] = coded[0:MAIN, d * LANES : (d + 1) * LANES].astype(jnp.bfloat16)
            extras += [high, coded[33:34], coded[35:37], halves]
        extras.append(jnp.zeros((1, wide), jnp.float32))
        extras = jnp.concatenate(extras, axis=0).astype(jnp.bfloat16)
        for d in range(many):
            out_ref[p * many + d, components * MAIN :] = extras[:, d * LANES : (d + 1) * LANES]
    root_ref[...] = jnp.sqrt(weight_ref[...])


def gram_kernel(steps_all, offsets, rows_ref, root_ref, out_ref, high_ref, low_ref):
    components = (rows_ref.shape[1] - 1) // (MAIN + EXTRA)
    extra = components * MAIN
    group = NF // 2
    rows = jnp.transpose(rows_ref[...].astype(jnp.float32), (1, 0, 2))
    root = root_ref[...]
    last = lax.broadcasted_iota(jnp.int32, (NH, LANES), 0) == NB
    for c in range(components):
        further = rows[extra + c * EXTRA : extra + (c + 1) * EXTRA]
        scale = jnp.exp2(further[4] * 0.5) * (1.0 / (STEEP * spread(c)))
        sums = further[0] + value_of(further[1], scale)
        delta = (sums * (1.0 / HALF) - jnp.sum(sums, axis=0, keepdims=True) * (1.0 / steps_all)) * root
        scale = scale * root

        def value(i, k):
            coded = rows[c * MAIN + i * NF + k - 1] if k <= NF else further[2 + i]
            return value_of(coded, scale) + (offsets[i][k] * delta if k % 2 else 0.0)

        for i in range(2):
            before, here = (delta * float(HALF), jnp.zeros_like(delta))[i], value(i, 1)
            for k in range(1, NF + 1):
                after = value(i, k + 1)
                sides, twice = before + after, here + here
                back = pltpu.roll(twice + sides, NH - 1, 0)
                spectrum = twice - sides - back if k % 2 else twice - sides + back
                spectrum = jnp.where(last, root if i == 0 and c == 0 else 0.0, spectrum)
                high = spectrum.astype(jnp.bfloat16)
                g, f = (k - 1) // group, (k - 1) % group
                at = pl.ds((i * group + f) * NH, NH)
                high_ref[g, at, c * LANES : (c + 1) * LANES] = high
                low_ref[g, at, c * LANES : (c + 1) * LANES] = (spectrum - high.astype(jnp.float32)).astype(jnp.bfloat16)
                before, here = here, after
    row = lax.broadcasted_iota(jnp.int32, (NH, LANES), 0)
    column = lax.broadcasted_iota(jnp.int32, (NH, LANES), 1) % NH
    shared = lax.broadcasted_iota(jnp.int32, (NH, LANES), 1) // NH
    dims = (((1,), (1,)), ((), ()))
    for g in range(2):
        high, low = high_ref[g], low_ref[g]
        left, right = jnp.concatenate([high, high, low], 1), jnp.concatenate([high, low, high], 1)
        gram = lax.dot_general(left, right, dims, preferred_element_type=jnp.float32)
        gram = gram.reshape(2, group, NH, gram.shape[1])
        kept = []
        for i, j in ((0, 0), (1, 1), (0, 1)):
            block = jnp.zeros(shared.shape, jnp.float32)
            for f in range(group):
                block = block + jnp.where(shared == f, gram[i, f, :, j * LANES : (j + 1) * LANES], 0.0)
            kept.append(block)
        out_ref[g, :, 0:LANES] = jnp.where(column >= row, kept[0], jnp.concatenate([kept[0][0:1], kept[1][:-1]], 0))
        out_ref[g, :, LANES:] = kept[2]


def transform(block, weights):
    table, _ = half_table()
    components, _, points = block.shape
    table = pieces(table)
    return pl.pallas_call(
        transform_kernel,
        in_specs=[pl.BlockSpec(memory_space=pltpu.HBM)] * 3,
        out_shape=(
            jax.ShapeDtypeStruct((points // LANES, components * (MAIN + EXTRA) + 1, LANES), jnp.bfloat16),
            jax.ShapeDtypeStruct((1, LANES), jnp.float32),
        ),
        scratch_shapes=[
            pltpu.VMEM(block.shape, block.dtype),
            pltpu.VMEM(table.shape, jnp.bfloat16),
            pltpu.VMEM((1, LANES), jnp.float32),
            pltpu.SemaphoreType.DMA((components + 2,)),
        ],
        compiler_params=pltpu.CompilerParams(vmem_limit_bytes=VMEM),
    )(*[pltpu.with_memory_space_constraint(x, pltpu.HBM) for x in (block, jnp.asarray(table), weights[None, :])])


def local_gram(rows, root, steps_all):
    _, offsets = half_table()
    width = (rows.shape[1] - 1) // (MAIN + EXTRA) * LANES
    return pl.pallas_call(
        lambda *refs: gram_kernel(steps_all, offsets, *refs),
        out_shape=jax.ShapeDtypeStruct((2, NH, 2 * LANES), jnp.float32),
        scratch_shapes=[pltpu.VMEM((2, NF * NH, width), jnp.bfloat16)] * 2,
        compiler_params=pltpu.CompilerParams(vmem_limit_bytes=VMEM),
    )(rows, root)


def partners(value, axis, size, steps):
    return [lax.ppermute(value, axis, [(i, i ^ step) for i in range(size)]) for step in steps]


def finish_kernel(*refs):
    out_ref = refs[-1]
    summed = refs[0][...]
    for ref in refs[1:-1]:
        summed = summed + ref[...]
    weight_sum = summed[0, NB : NB + 1, NB : NB + 1]
    summed = summed * (1.0 / (16.0 * 0.375 * NFFT)) / weight_sum
    cut, turned = [], []
    for which in range(2):
        half = summed[:, :, which * LANES : (which + 1) * LANES]
        cut.append(jnp.stack([half[g][:, f * NH : (f + 1) * NH] for g in range(2) for f in range(NF // 2)]))
        turned.append(jnp.concatenate([half[g].T.reshape(NF // 2, NH, NH) for g in range(2)], axis=0))
    row = lax.broadcasted_iota(jnp.int32, (NF, NB, NB), 1)
    column = lax.broadcasted_iota(jnp.int32, (NF, NB, NB), 2)
    re_re = jnp.where(row <= column, cut[0][:, 0:NB, 0:NB], turned[0][:, 0:NB, 0:NB])
    im_im = jnp.where(row >= column, cut[0][:, 1:NH, 0:NB], turned[0][:, 0:NB, 1:NH])
    upper = jnp.concatenate([re_re, cut[1][:, 0:NB, 0:NB]], axis=2)
    lower = jnp.concatenate([turned[1][:, 0:NB, 0:NB], im_im], axis=2)
    out_ref[0:NB] = jnp.transpose(upper, (1, 0, 2))
    out_ref[NB:] = jnp.transpose(lower, (1, 0, 2))


def finish(terms):
    out = pl.pallas_call(
        finish_kernel,
        out_shape=jax.ShapeDtypeStruct((2 * NB, NF, 2 * NB), jnp.float32),
        compiler_params=pltpu.CompilerParams(vmem_limit_bytes=VMEM),
    )(*terms)
    return jnp.transpose(out, (1, 0, 2))


def sum_over(value, axis, size):
    rounds, step = [], 1
    while step < size:
        wide = step == 2 and 4 * step <= size
        rounds.append([c + (step > 1) for c in ([step, 2 * step, 3 * step] if wide else [step])])
        step *= 4 if wide else 2
    for steps in rounds[:-1]:
        value = sum(partners(value, axis, size, steps), value)
    return [value] + partners(value, axis, size, rounds[-1])


def make_local(n_space):
    def local(snapshots, weights):
        steps, components, points = snapshots.shape
        share = HALF // steps
        block = jnp.transpose(snapshots, (1, 0, 2))
        across = None
        if share > 1:
            block = block.reshape(components, steps, NH, share, -1)
            teams = [[h * share + i for i in range(share)] for h in range(NH)]
            block = lax.all_to_all(block, "space", split_axis=3, concat_axis=1, axis_index_groups=teams, tiled=True)
            block = block.reshape(components, HALF, -1)
            across = [[h * share + i for h in range(NH)] for i in range(share)]
        rows, root = transform(block, weights)
        rows = lax.all_to_all(rows, "space", split_axis=0, concat_axis=0, axis_index_groups=across, tiled=True)
        gram = local_gram(rows, root, n_space * steps)
        return finish(sum_over(gram, "space", n_space))

    return local


def solution(mesh):
    in_specs = (P(("grp", "space"), None, None), P(("grp", "space")))
    out_specs = P("grp", None, None)
    return jax.shard_map(
        make_local(mesh.shape["space"]), mesh=mesh, in_specs=in_specs, out_specs=out_specs, check_vma=False
    )
```

```python
import numpy as np
import ml_dtypes
import jax
import jax.numpy as jnp
from jax import lax
from jax.experimental import pallas as pl
from jax.experimental.pallas import tpu as pltpu
from jax.sharding import PartitionSpec as P

NFFT = 128
NB = 15
NF = 16
HALF = NFFT // 2
NH = NB + 1
LANES = 128
MAIN = 2 * NF
EXTRA = 5
ROWS = 40
SMALLEST = 2.0**-60
VMEM = 48 * 1024 * 1024


def half_table():
    turns = 2.0 * np.pi * np.arange(NF + 2)[:, None] * np.arange(HALF)[None, :] / NFFT
    re, im = np.cos(turns), -np.sin(turns)
    offset_re, offset_im = re.sum(1), im.sum(1)
    re0, im0 = re - re.mean(1, keepdims=True), im - im.mean(1, keepdims=True)
    table = np.zeros((ROWS, HALF))
    table[0:NF] = re0[1 : NF + 1]
    table[NF : 2 * NF] = im0[1 : NF + 1]
    table[32] = 1.0
    table[35] = re0[NF + 1]
    table[36] = im0[NF + 1]
    return table, (offset_re.tolist(), offset_im.tolist())


def pieces(table):
    high = table.astype(ml_dtypes.bfloat16)
    low = (table - high.astype(np.float64)).astype(ml_dtypes.bfloat16)
    for row in range(table.shape[0]):
        for _ in range(8):
            left = table[row].sum() - high[row].astype(np.float64).sum() - low[row].astype(np.float64).sum()
            moved = (low[row].astype(np.float64) + left).astype(ml_dtypes.bfloat16)
            error = np.abs(moved.astype(np.float64) - low[row].astype(np.float64) - left)
            at = int(np.argmin(error))
            if error[at] >= abs(left):
                break
            low[row, at] = moved[at]
    return np.concatenate([high, low], axis=1)


def spread(component):
    place = lax.broadcasted_iota(jnp.int32, (1, LANES), 1) + LANES * component
    turns = place.astype(jnp.float32) * 0.618034
    return 1.0 / (1.0 + 0.125 * (turns - jnp.floor(turns)))


def transform_kernel(block_hbm, table_hbm, weight_hbm, out_ref, root_ref, block_ref, table_ref, weight_ref, sems):
    components, _, points = block_ref.shape
    copies = [pltpu.make_async_copy(block_hbm.at[c], block_ref.at[c], sems.at[c]) for c in range(components)]
    copies.append(pltpu.make_async_copy(table_hbm, table_ref, sems.at[components]))
    copies.append(pltpu.make_async_copy(weight_hbm, weight_ref, sems.at[components + 1]))
    for copy in copies:
        copy.start()
    for copy in copies:
        copy.wait()
    table = table_ref[...]
    top = jnp.max(jnp.abs(block_ref[...].astype(jnp.float32)), axis=(0, 1, 2), keepdims=True)[0]
    power = jnp.floor(jnp.log2(jnp.maximum(top, SMALLEST)))
    extras = []
    for c in range(components):
        block = block_ref[c]
        rows = jnp.dot(table, jnp.concatenate([block] * 2, axis=0), preferred_element_type=jnp.float32)
        scale = jnp.concatenate([jnp.exp2(7.0 - power) * spread(c)] * (points // LANES), axis=1)
        rows = rows * scale
        for d in range(points // LANES):
            out_ref[d, c * MAIN : (c + 1) * MAIN] = rows[0:MAIN, d * LANES : (d + 1) * LANES]
        shifted = rows[32:33] * 8193.0
        high = shifted - (shifted - rows[32:33])
        extras += [high, rows[32:33] - high, rows[35:37], jnp.broadcast_to(power, (1, points))]
    extras.append(jnp.zeros((1, points), jnp.float32))
    extras = jnp.concatenate(extras, axis=0)
    for d in range(points // LANES):
        out_ref[d, components * MAIN :] = extras[:, d * LANES : (d + 1) * LANES]
    root_ref[...] = jnp.sqrt(weight_ref[...])


def gram_kernel(steps_all, offsets, rows_ref, root_ref, out_ref, high_ref, low_ref):
    components = (rows_ref.shape[1] - 1) // (MAIN + EXTRA)
    extra = components * MAIN
    group = NF // 2
    rows = jnp.transpose(rows_ref[...], (1, 0, 2))
    root = root_ref[...]
    last = lax.broadcasted_iota(jnp.int32, (NH, LANES), 0) == NB
    for c in range(components):
        further = rows[extra + c * EXTRA : extra + (c + 1) * EXTRA]
        scale = jnp.exp2(further[4] - 7.0) * (1.0 / spread(c))
        sums = (further[0] + further[1]) * scale
        delta = (sums * (1.0 / HALF) - jnp.sum(sums, axis=0, keepdims=True) * (1.0 / steps_all)) * root
        scale = scale * root

        def value(i, k):
            coded = rows[c * MAIN + i * NF + k - 1] if k <= NF else further[2 + i]
            part = coded * scale
            return part + offsets[i][k] * delta if k % 2 else part

        for i in range(2):
            before, here = (delta * float(HALF), jnp.zeros_like(delta))[i], value(i, 1)
            for k in range(1, NF + 1):
                after = value(i, k + 1)
                sides, twice = before + after, here + here
                back = pltpu.roll(twice + sides, NH - 1, 0)
                spectrum = twice - sides - back if k % 2 else twice - sides + back
                spectrum = jnp.where(last, root if i == 0 and c == 0 else 0.0, spectrum)
                high = spectrum.astype(jnp.bfloat16)
                g, f = (k - 1) // group, (k - 1) % group
                at = pl.ds((i * group + f) * NH, NH)
                high_ref[g, at, c * LANES : (c + 1) * LANES] = high
                low_ref[g, at, c * LANES : (c + 1) * LANES] = (spectrum - high.astype(jnp.float32)).astype(jnp.bfloat16)
                before, here = here, after
    row = lax.broadcasted_iota(jnp.int32, (NH, LANES), 0)
    column = lax.broadcasted_iota(jnp.int32, (NH, LANES), 1) % NH
    shared = lax.broadcasted_iota(jnp.int32, (NH, LANES), 1) // NH
    dims = (((1,), (1,)), ((), ()))
    for g in range(2):
        high, low = high_ref[g], low_ref[g]
        left, right = jnp.concatenate([high, high, low], 1), jnp.concatenate([high, low, high], 1)
        gram = lax.dot_general(left, right, dims, preferred_element_type=jnp.float32)
        gram = gram.reshape(2, group, NH, gram.shape[1])
        kept = []
        for i, j in ((0, 0), (1, 1), (0, 1)):
            block = jnp.zeros(shared.shape, jnp.float32)
            for f in range(group):
                block = block + jnp.where(shared == f, gram[i, f, :, j * LANES : (j + 1) * LANES], 0.0)
            kept.append(block)
        out_ref[g, :, 0:LANES] = jnp.where(column >= row, kept[0], jnp.concatenate([kept[0][0:1], kept[1][:-1]], 0))
        out_ref[g, :, LANES:] = kept[2]


def transform(block, weights):
    table, _ = half_table()
    components, _, points = block.shape
    table = pieces(table)
    return pl.pallas_call(
        transform_kernel,
        in_specs=[pl.BlockSpec(memory_space=pltpu.HBM)] * 3,
        out_shape=(
            jax.ShapeDtypeStruct((points // LANES, components * (MAIN + EXTRA) + 1, LANES), jnp.float32),
            jax.ShapeDtypeStruct((1, LANES), jnp.float32),
        ),
        scratch_shapes=[
            pltpu.VMEM(block.shape, block.dtype),
            pltpu.VMEM(table.shape, jnp.bfloat16),
            pltpu.VMEM((1, LANES), jnp.float32),
            pltpu.SemaphoreType.DMA((components + 2,)),
        ],
        compiler_params=pltpu.CompilerParams(vmem_limit_bytes=VMEM),
    )(*[pltpu.with_memory_space_constraint(x, pltpu.HBM) for x in (block, jnp.asarray(table), weights[None, :])])


def local_gram(rows, root, steps_all):
    _, offsets = half_table()
    width = (rows.shape[1] - 1) // (MAIN + EXTRA) * LANES
    return pl.pallas_call(
        lambda *refs: gram_kernel(steps_all, offsets, *refs),
        out_shape=jax.ShapeDtypeStruct((2, NH, 2 * LANES), jnp.float32),
        scratch_shapes=[pltpu.VMEM((2, NF * NH, width), jnp.bfloat16)] * 2,
        compiler_params=pltpu.CompilerParams(vmem_limit_bytes=VMEM),
    )(rows, root)


def partners(value, axis, size, steps):
    return [lax.ppermute(value, axis, [(i, i ^ step) for i in range(size)]) for step in steps]


def finish_kernel(*refs):
    out_ref = refs[-1]
    summed = refs[0][...]
    for ref in refs[1:-1]:
        summed = summed + ref[...]
    weight_sum = summed[0, NB : NB + 1, NB : NB + 1]
    summed = summed * (1.0 / (16.0 * 0.375 * NFFT)) / weight_sum
    cut, turned = [], []
    for which in range(2):
        half = summed[:, :, which * LANES : (which + 1) * LANES]
        cut.append(jnp.stack([half[g][:, f * NH : (f + 1) * NH] for g in range(2) for f in range(NF // 2)]))
        turned.append(jnp.concatenate([half[g].T.reshape(NF // 2, NH, NH) for g in range(2)], axis=0))
    row = lax.broadcasted_iota(jnp.int32, (NF, NB, NB), 1)
    column = lax.broadcasted_iota(jnp.int32, (NF, NB, NB), 2)
    re_re = jnp.where(row <= column, cut[0][:, 0:NB, 0:NB], turned[0][:, 0:NB, 0:NB])
    im_im = jnp.where(row >= column, cut[0][:, 1:NH, 0:NB], turned[0][:, 0:NB, 1:NH])
    upper = jnp.concatenate([re_re, cut[1][:, 0:NB, 0:NB]], axis=2)
    lower = jnp.concatenate([turned[1][:, 0:NB, 0:NB], im_im], axis=2)
    out_ref[0:NB] = jnp.transpose(upper, (1, 0, 2))
    out_ref[NB:] = jnp.transpose(lower, (1, 0, 2))


def finish(terms):
    out = pl.pallas_call(
        finish_kernel,
        out_shape=jax.ShapeDtypeStruct((2 * NB, NF, 2 * NB), jnp.float32),
        compiler_params=pltpu.CompilerParams(vmem_limit_bytes=VMEM),
    )(*terms)
    return jnp.transpose(out, (1, 0, 2))


def sum_over(value, axis, size):
    rounds, step = [], 1
    while step < size:
        wide = step == 2 and 4 * step <= size
        rounds.append([c + (step > 1) for c in ([step, 2 * step, 3 * step] if wide else [step])])
        step *= 4 if wide else 2
    for steps in rounds[:-1]:
        value = sum(partners(value, axis, size, steps), value)
    return [value] + partners(value, axis, size, rounds[-1])


def make_local(n_space):
    def local(snapshots, weights):
        steps, components, points = snapshots.shape
        share = HALF // steps
        block = jnp.transpose(snapshots, (1, 0, 2))
        across = None
        if share > 1:
            block = block.reshape(components, steps, NH, share, -1)
            teams = [[h * share + i for i in range(share)] for h in range(NH)]
            block = lax.all_to_all(block, "space", split_axis=3, concat_axis=1, axis_index_groups=teams, tiled=True)
            block = block.reshape(components, HALF, -1)
            across = [[h * share + i for h in range(NH)] for i in range(share)]
        rows, root = transform(block, weights)
        rows = lax.all_to_all(
            rows.astype(jnp.float16), "space", split_axis=0, concat_axis=0, axis_index_groups=across, tiled=True
        )
        gram = local_gram(rows.astype(jnp.float32), root, n_space * steps)
        return finish(sum_over(gram, "space", n_space))

    return local


def solution(mesh):
    in_specs = (P(("grp", "space"), None, None), P(("grp", "space")))
    out_specs = P("grp", None, None)
    return jax.shard_map(
        make_local(mesh.shape["space"]), mesh=mesh, in_specs=in_specs, out_specs=out_specs, check_vma=False
    )
```

```python
import math

import numpy as np
import ml_dtypes
import jax
import jax.numpy as jnp
from jax import lax
from jax.experimental import pallas as pl
from jax.experimental.pallas import tpu as pltpu
from jax.sharding import PartitionSpec as P

NFFT = 128
NB = 15
NF = 16
HALF = NFFT // 2
NH = NB + 1
LANES = 128
ORDER = (11, 10, 5, 4, 12, 15, 2, 14, 9, 13, 7, 1, 0, 6, 8, 3)
MAIN = 2 * NF
EXTRA = 5
ROWS = 40
SMALLEST = 2.0**-60
SMALL_SUM = 256.0
LOWEST, STEEP = -125.0, 251.0
VMEM = 48 * 1024 * 1024


def half_table():
    turns = 2.0 * np.pi * np.arange(NF + 2)[:, None] * np.arange(HALF)[None, :] / NFFT
    re, im = np.cos(turns), -np.sin(turns)
    offset_re, offset_im = re.sum(1), im.sum(1)
    re0, im0 = re - re.mean(1, keepdims=True), im - im.mean(1, keepdims=True)
    table = np.zeros((ROWS, HALF))
    table[0:NF] = re0[1 : NF + 1]
    table[NF : 2 * NF] = im0[1 : NF + 1]
    table[32] = 1.0 / SMALL_SUM
    table[35] = re0[NF + 1]
    table[36] = im0[NF + 1]
    return table, (offset_re.tolist(), offset_im.tolist())


def pieces(table):
    high = table.astype(ml_dtypes.bfloat16)
    low = (table - high.astype(np.float64)).astype(ml_dtypes.bfloat16)
    for row in range(table.shape[0]):
        for _ in range(8):
            left = table[row].sum() - high[row].astype(np.float64).sum() - low[row].astype(np.float64).sum()
            moved = (low[row].astype(np.float64) + left).astype(ml_dtypes.bfloat16)
            error = np.abs(moved.astype(np.float64) - low[row].astype(np.float64) - left)
            at = int(np.argmin(error))
            if error[at] >= abs(left):
                break
            low[row, at] = moved[at]
    return np.concatenate([high, low], axis=1)


def spread(component):
    place = lax.broadcasted_iota(jnp.int32, (1, LANES), 1) + LANES * component
    turns = place.astype(jnp.float32) * 0.618034
    return 1.0 / (1.0 + 0.125 * (turns - jnp.floor(turns)))


def coded_of(values, sizes, scale):
    coded = jnp.exp2(sizes * (scale * STEEP) + LOWEST)
    return jnp.where(values < 0.0, -coded, coded)


def value_of(coded, scale):
    return (jnp.log2(jnp.abs(coded)) - LOWEST) * jnp.where(coded < 0.0, -scale, scale)


def transform_kernel(block_hbm, table_hbm, weight_hbm, out_ref, root_ref, block_ref, table_ref, weight_ref, sems):
    components, _, points = block_ref.shape
    copies = [pltpu.make_async_copy(block_hbm.at[c], block_ref.at[c], sems.at[c]) for c in range(components)]
    copies.append(pltpu.make_async_copy(table_hbm, table_ref, sems.at[components]))
    copies.append(pltpu.make_async_copy(weight_hbm, weight_ref, sems.at[components + 1]))
    for copy in copies:
        copy.start()
    for copy in copies:
        copy.wait()
    table = table_ref[...]
    place = lax.broadcasted_iota(jnp.int32, (8, 1), 0)
    place_of = [ORDER.index(h) for h in range(points // LANES)]
    many = math.gcd(points // LANES, 4)
    wide = many * LANES
    for p in range(points // wide):
        extras = []
        for c in range(components):
            block = block_ref[c, :, p * wide : (p + 1) * wide]
            rows = jnp.dot(table, jnp.concatenate([block] * 2, axis=0), preferred_element_type=jnp.float32)
            sizes = jnp.abs(rows)
            top = sizes[:, 0:LANES]
            for d in range(1, many):
                top = jnp.maximum(top, sizes[:, d * LANES : (d + 1) * LANES])
            halves = jnp.ceil(2.0 * jnp.log2(jnp.maximum(jnp.max(top, axis=0, keepdims=True), SMALLEST)))
            scale = jnp.exp2(halves * -0.5) * spread(c)
            scale, halves = (jnp.concatenate([x] * many, axis=1) for x in (scale, halves))
            whole = rows[32:33] * SMALL_SUM
            high = whole.astype(jnp.bfloat16).astype(jnp.float32)
            rows = jnp.concatenate([rows[0:32], jnp.where(place == 1, whole - high, rows[32:40])], axis=0)
            coded = coded_of(rows, jnp.abs(rows), scale)
            for d in range(many):
                out_ref[place_of[p * many + d], c * MAIN : (c + 1) * MAIN] = coded[0:MAIN, d * LANES : (d + 1) * LANES].astype(jnp.bfloat16)
            extras += [high, coded[33:34], coded[35:37], halves]
        extras.append(jnp.zeros((1, wide), jnp.float32))
        extras = jnp.concatenate(extras, axis=0).astype(jnp.bfloat16)
        for d in range(many):
            out_ref[place_of[p * many + d], components * MAIN :] = extras[:, d * LANES : (d + 1) * LANES]
    root_ref[...] = jnp.sqrt(weight_ref[...])


def gram_kernel(steps_all, offsets, rows_ref, root_ref, out_ref, high_ref, low_ref):
    components = (rows_ref.shape[1] - 1) // (MAIN + EXTRA)
    extra = components * MAIN
    group = NF // 2
    rows = jnp.stack([rows_ref[ORDER.index(h)] for h in range(NH)])
    rows = jnp.transpose(rows.astype(jnp.float32), (1, 0, 2))
    root = root_ref[...]
    last = lax.broadcasted_iota(jnp.int32, (NH, LANES), 0) == NB
    for c in range(components):
        further = rows[extra + c * EXTRA : extra + (c + 1) * EXTRA]
        scale = jnp.exp2(further[4] * 0.5) * (1.0 / (STEEP * spread(c)))
        sums = further[0] + value_of(further[1], scale)
        delta = (sums * (1.0 / HALF) - jnp.sum(sums, axis=0, keepdims=True) * (1.0 / steps_all)) * root
        scale = scale * root

        def value(i, k):
            coded = rows[c * MAIN + i * NF + k - 1] if k <= NF else further[2 + i]
            return value_of(coded, scale) + (offsets[i][k] * delta if k % 2 else 0.0)

        for i in range(2):
            before, here = (delta * float(HALF), jnp.zeros_like(delta))[i], value(i, 1)
            for k in range(1, NF + 1):
                after = value(i, k + 1)
                sides, twice = before + after, here + here
                back = pltpu.roll(twice + sides, NH - 1, 0)
                spectrum = twice - sides - back if k % 2 else twice - sides + back
                spectrum = jnp.where(last, root if i == 0 and c == 0 else 0.0, spectrum)
                high = spectrum.astype(jnp.bfloat16)
                g, f = (k - 1) // group, (k - 1) % group
                at = pl.ds((i * group + f) * NH, NH)
                high_ref[g, at, c * LANES : (c + 1) * LANES] = high
                low_ref[g, at, c * LANES : (c + 1) * LANES] = (spectrum - high.astype(jnp.float32)).astype(jnp.bfloat16)
                before, here = here, after
    row = lax.broadcasted_iota(jnp.int32, (NH, LANES), 0)
    column = lax.broadcasted_iota(jnp.int32, (NH, LANES), 1) % NH
    shared = lax.broadcasted_iota(jnp.int32, (NH, LANES), 1) // NH
    dims = (((1,), (1,)), ((), ()))
    for g in range(2):
        high, low = high_ref[g], low_ref[g]
        left, right = jnp.concatenate([high, high, low], 1), jnp.concatenate([high, low, high], 1)
        gram = lax.dot_general(left, right, dims, preferred_element_type=jnp.float32)
        gram = gram.reshape(2, group, NH, gram.shape[1])
        kept = []
        for i, j in ((0, 0), (1, 1), (0, 1)):
            block = jnp.zeros(shared.shape, jnp.float32)
            for f in range(group):
                block = block + jnp.where(shared == f, gram[i, f, :, j * LANES : (j + 1) * LANES], 0.0)
            kept.append(block)
        out_ref[g, :, 0:LANES] = jnp.where(column >= row, kept[0], jnp.concatenate([kept[0][0:1], kept[1][:-1]], 0))
        out_ref[g, :, LANES:] = kept[2]


def transform(block, weights):
    table, _ = half_table()
    components, _, points = block.shape
    table = pieces(table)
    return pl.pallas_call(
        transform_kernel,
        in_specs=[pl.BlockSpec(memory_space=pltpu.HBM)] * 3,
        out_shape=(
            jax.ShapeDtypeStruct((points // LANES, components * (MAIN + EXTRA) + 1, LANES), jnp.bfloat16),
            jax.ShapeDtypeStruct((1, LANES), jnp.float32),
        ),
        scratch_shapes=[
            pltpu.VMEM(block.shape, block.dtype),
            pltpu.VMEM(table.shape, jnp.bfloat16),
            pltpu.VMEM((1, LANES), jnp.float32),
            pltpu.SemaphoreType.DMA((components + 2,)),
        ],
        compiler_params=pltpu.CompilerParams(vmem_limit_bytes=VMEM),
    )(*[pltpu.with_memory_space_constraint(x, pltpu.HBM) for x in (block, jnp.asarray(table), weights[None, :])])


def local_gram(rows, root, steps_all):
    _, offsets = half_table()
    width = (rows.shape[1] - 1) // (MAIN + EXTRA) * LANES
    return pl.pallas_call(
        lambda *refs: gram_kernel(steps_all, offsets, *refs),
        out_shape=jax.ShapeDtypeStruct((2, NH, 2 * LANES), jnp.float32),
        scratch_shapes=[pltpu.VMEM((2, NF * NH, width), jnp.bfloat16)] * 2,
        compiler_params=pltpu.CompilerParams(vmem_limit_bytes=VMEM),
    )(rows, root)


def partners(value, axis, size, steps):
    return [lax.ppermute(value, axis, [(i, i ^ step) for i in range(size)]) for step in steps]


def finish_kernel(*refs):
    out_ref = refs[-1]
    summed = refs[0][...]
    for ref in refs[1:-1]:
        summed = summed + ref[...]
    weight_sum = summed[0, NB : NB + 1, NB : NB + 1]
    summed = summed * (1.0 / (16.0 * 0.375 * NFFT)) / weight_sum
    cut, turned = [], []
    for which in range(2):
        half = summed[:, :, which * LANES : (which + 1) * LANES]
        cut.append(jnp.stack([half[g][:, f * NH : (f + 1) * NH] for g in range(2) for f in range(NF // 2)]))
        turned.append(jnp.concatenate([half[g].T.reshape(NF // 2, NH, NH) for g in range(2)], axis=0))
    row = lax.broadcasted_iota(jnp.int32, (NF, NB, NB), 1)
    column = lax.broadcasted_iota(jnp.int32, (NF, NB, NB), 2)
    re_re = jnp.where(row <= column, cut[0][:, 0:NB, 0:NB], turned[0][:, 0:NB, 0:NB])
    im_im = jnp.where(row >= column, cut[0][:, 1:NH, 0:NB], turned[0][:, 0:NB, 1:NH])
    upper = jnp.concatenate([re_re, cut[1][:, 0:NB, 0:NB]], axis=2)
    lower = jnp.concatenate([turned[1][:, 0:NB, 0:NB], im_im], axis=2)
    out_ref[0:NB] = jnp.transpose(upper, (1, 0, 2))
    out_ref[NB:] = jnp.transpose(lower, (1, 0, 2))


def finish(terms):
    out = pl.pallas_call(
        finish_kernel,
        out_shape=jax.ShapeDtypeStruct((2 * NB, NF, 2 * NB), jnp.float32),
        compiler_params=pltpu.CompilerParams(vmem_limit_bytes=VMEM),
    )(*terms)
    return jnp.transpose(out, (1, 0, 2))


def sum_over(value, axis, size):
    rounds, step = [], 1
    while step < size:
        wide = step == 2 and 4 * step <= size
        rounds.append([c + (step > 1) for c in ([step, 2 * step, 3 * step] if wide else [step])])
        step *= 4 if wide else 2
    for steps in rounds[:-1]:
        value = sum(partners(value, axis, size, steps), value)
    return [value] + partners(value, axis, size, rounds[-1])


def make_local(n_space):
    def local(snapshots, weights):
        steps, components, points = snapshots.shape
        share = HALF // steps
        block = jnp.transpose(snapshots, (1, 0, 2))
        across = [[h * share + i for h in ORDER] for i in range(share)]
        if share > 1:
            block = block.reshape(components, steps, NH, share, -1)
            teams = [[h * share + i for i in range(share)] for h in range(NH)]
            block = lax.all_to_all(block, "space", split_axis=3, concat_axis=1, axis_index_groups=teams, tiled=True)
            block = block.reshape(components, HALF, -1)
        rows, root = transform(block, weights)
        rows = lax.all_to_all(rows, "space", split_axis=0, concat_axis=0, axis_index_groups=across, tiled=True)
        gram = local_gram(rows, root, n_space * steps)
        return finish(sum_over(gram, "space", n_space))

    return local


def solution(mesh):
    in_specs = (P(("grp", "space"), None, None), P(("grp", "space")))
    out_specs = P("grp", None, None)
    return jax.shard_map(
        make_local(mesh.shape["space"]), mesh=mesh, in_specs=in_specs, out_specs=out_specs, check_vma=False
    )
```

```python
import math

import numpy as np
import ml_dtypes
import jax
import jax.numpy as jnp
from jax import lax
from jax.experimental import pallas as pl
from jax.experimental.pallas import tpu as pltpu
from jax.sharding import PartitionSpec as P

NFFT = 128
NB = 15
NF = 16
HALF = NFFT // 2
NH = NB + 1
LANES = 128
ORDER = (11, 10, 7, 6, 15, 12, 2, 14, 9, 0, 1, 5, 13, 4, 8, 3)
MAIN = 2 * NF
EXTRA = 5
ROWS = 40
SMALLEST = 2.0**-60
SMALL_SUM = 256.0
LOWEST, STEEP = -125.0, 251.0
VMEM = 48 * 1024 * 1024


def half_table():
    turns = 2.0 * np.pi * np.arange(NF + 2)[:, None] * np.arange(HALF)[None, :] / NFFT
    re, im = np.cos(turns), -np.sin(turns)
    offset_re, offset_im = re.sum(1), im.sum(1)
    re0, im0 = re - re.mean(1, keepdims=True), im - im.mean(1, keepdims=True)
    table = np.zeros((ROWS, HALF))
    table[0:NF] = re0[1 : NF + 1]
    table[NF : 2 * NF] = im0[1 : NF + 1]
    table[32] = 1.0 / SMALL_SUM
    table[35] = re0[NF + 1]
    table[36] = im0[NF + 1]
    return table, (offset_re.tolist(), offset_im.tolist())


def pieces(table):
    high = table.astype(ml_dtypes.bfloat16)
    low = (table - high.astype(np.float64)).astype(ml_dtypes.bfloat16)
    for row in range(table.shape[0]):
        for _ in range(8):
            left = table[row].sum() - high[row].astype(np.float64).sum() - low[row].astype(np.float64).sum()
            moved = (low[row].astype(np.float64) + left).astype(ml_dtypes.bfloat16)
            error = np.abs(moved.astype(np.float64) - low[row].astype(np.float64) - left)
            at = int(np.argmin(error))
            if error[at] >= abs(left):
                break
            low[row, at] = moved[at]
    return np.concatenate([high, low], axis=1)


def spread(component):
    place = lax.broadcasted_iota(jnp.int32, (1, LANES), 1) + LANES * component
    turns = place.astype(jnp.float32) * 0.618034
    return 1.0 / (1.0 + 0.125 * (turns - jnp.floor(turns)))


def coded_of(values, sizes, scale):
    coded = jnp.exp2(sizes * (scale * STEEP) + LOWEST)
    return jnp.where(values < 0.0, -coded, coded)


def value_of(coded, scale):
    return (jnp.log2(jnp.abs(coded)) - LOWEST) * jnp.where(coded < 0.0, -scale, scale)


def transform_kernel(block_hbm, table_hbm, weight_hbm, out_ref, root_ref, block_ref, table_ref, weight_ref, sems):
    components, _, points = block_ref.shape
    copies = [pltpu.make_async_copy(block_hbm.at[c], block_ref.at[c], sems.at[c]) for c in range(components)]
    copies.append(pltpu.make_async_copy(table_hbm, table_ref, sems.at[components]))
    copies.append(pltpu.make_async_copy(weight_hbm, weight_ref, sems.at[components + 1]))
    for copy in copies:
        copy.start()
    for copy in copies:
        copy.wait()
    table = table_ref[...]
    place = lax.broadcasted_iota(jnp.int32, (8, 1), 0)
    place_of = [ORDER.index(h) for h in range(points // LANES)]
    many = math.gcd(points // LANES, 4)
    wide = many * LANES
    for p in range(points // wide):
        extras = []
        for c in range(components):
            block = block_ref[c, :, p * wide : (p + 1) * wide]
            rows = jnp.dot(table, jnp.concatenate([block] * 2, axis=0), preferred_element_type=jnp.float32)
            sizes = jnp.abs(rows)
            top = sizes[:, 0:LANES]
            for d in range(1, many):
                top = jnp.maximum(top, sizes[:, d * LANES : (d + 1) * LANES])
            halves = jnp.ceil(2.0 * jnp.log2(jnp.maximum(jnp.max(top, axis=0, keepdims=True), SMALLEST)))
            scale = jnp.exp2(halves * -0.5) * spread(c)
            scale, halves = (jnp.concatenate([x] * many, axis=1) for x in (scale, halves))
            whole = rows[32:33] * SMALL_SUM
            high = whole.astype(jnp.bfloat16).astype(jnp.float32)
            rows = jnp.concatenate([rows[0:32], jnp.where(place == 1, whole - high, rows[32:40])], axis=0)
            coded = coded_of(rows, jnp.abs(rows), scale)
            for d in range(many):
                out_ref[place_of[p * many + d], c * MAIN : (c + 1) * MAIN] = coded[0:MAIN, d * LANES : (d + 1) * LANES].astype(jnp.bfloat16)
            extras += [high, coded[33:34], coded[35:37], halves]
        extras.append(jnp.zeros((1, wide), jnp.float32))
        extras = jnp.concatenate(extras, axis=0).astype(jnp.bfloat16)
        for d in range(many):
            out_ref[place_of[p * many + d], components * MAIN :] = extras[:, d * LANES : (d + 1) * LANES]
    root_ref[...] = jnp.sqrt(weight_ref[...])


def gram_kernel(steps_all, offsets, rows_ref, root_ref, out_ref, high_ref, low_ref):
    components = (rows_ref.shape[1] - 1) // (MAIN + EXTRA)
    extra = components * MAIN
    group = NF // 2
    rows = jnp.stack([rows_ref[ORDER.index(h)] for h in range(NH)])
    rows = jnp.transpose(rows.astype(jnp.float32), (1, 0, 2))
    root = root_ref[...]
    last = lax.broadcasted_iota(jnp.int32, (NH, LANES), 0) == NB
    for c in range(components):
        further = rows[extra + c * EXTRA : extra + (c + 1) * EXTRA]
        scale = jnp.exp2(further[4] * 0.5) * (1.0 / (STEEP * spread(c)))
        sums = further[0] + value_of(further[1], scale)
        delta = (sums * (1.0 / HALF) - jnp.sum(sums, axis=0, keepdims=True) * (1.0 / steps_all)) * root
        scale = scale * root

        def value(i, k):
            coded = rows[c * MAIN + i * NF + k - 1] if k <= NF else further[2 + i]
            return value_of(coded, scale) + (offsets[i][k] * delta if k % 2 else 0.0)

        for i in range(2):
            before, here = (delta * float(HALF), jnp.zeros_like(delta))[i], value(i, 1)
            for k in range(1, NF + 1):
                after = value(i, k + 1)
                sides, twice = before + after, here + here
                back = pltpu.roll(twice + sides, NH - 1, 0)
                spectrum = twice - sides - back if k % 2 else twice - sides + back
                spectrum = jnp.where(last, root if i == 0 and c == 0 else 0.0, spectrum)
                high = spectrum.astype(jnp.bfloat16)
                g, f = (k - 1) // group, (k - 1) % group
                at = pl.ds((i * group + f) * NH, NH)
                high_ref[g, at, c * LANES : (c + 1) * LANES] = high
                low_ref[g, at, c * LANES : (c + 1) * LANES] = (spectrum - high.astype(jnp.float32)).astype(jnp.bfloat16)
                before, here = here, after
    row = lax.broadcasted_iota(jnp.int32, (NH, LANES), 0)
    column = lax.broadcasted_iota(jnp.int32, (NH, LANES), 1) % NH
    shared = lax.broadcasted_iota(jnp.int32, (NH, LANES), 1) // NH
    dims = (((1,), (1,)), ((), ()))
    for g in range(2):
        high, low = high_ref[g], low_ref[g]
        left, right = jnp.concatenate([high, high, low], 1), jnp.concatenate([high, low, high], 1)
        gram = lax.dot_general(left, right, dims, preferred_element_type=jnp.float32)
        gram = gram.reshape(2, group, NH, gram.shape[1])
        kept = []
        for i, j in ((0, 0), (1, 1), (0, 1)):
            block = jnp.zeros(shared.shape, jnp.float32)
            for f in range(group):
                block = block + jnp.where(shared == f, gram[i, f, :, j * LANES : (j + 1) * LANES], 0.0)
            kept.append(block)
        out_ref[g, :, 0:LANES] = jnp.where(column >= row, kept[0], jnp.concatenate([kept[0][0:1], kept[1][:-1]], 0))
        out_ref[g, :, LANES:] = kept[2]


def transform(block, weights):
    table, _ = half_table()
    components, _, points = block.shape
    table = pieces(table)
    return pl.pallas_call(
        transform_kernel,
        in_specs=[pl.BlockSpec(memory_space=pltpu.HBM)] * 3,
        out_shape=(
            jax.ShapeDtypeStruct((points // LANES, components * (MAIN + EXTRA) + 1, LANES), jnp.bfloat16),
            jax.ShapeDtypeStruct((1, LANES), jnp.float32),
        ),
        scratch_shapes=[
            pltpu.VMEM(block.shape, block.dtype),
            pltpu.VMEM(table.shape, jnp.bfloat16),
            pltpu.VMEM((1, LANES), jnp.float32),
            pltpu.SemaphoreType.DMA((components + 2,)),
        ],
        compiler_params=pltpu.CompilerParams(vmem_limit_bytes=VMEM),
    )(*[pltpu.with_memory_space_constraint(x, pltpu.HBM) for x in (block, jnp.asarray(table), weights[None, :])])


def local_gram(rows, root, steps_all):
    _, offsets = half_table()
    width = (rows.shape[1] - 1) // (MAIN + EXTRA) * LANES
    return pl.pallas_call(
        lambda *refs: gram_kernel(steps_all, offsets, *refs),
        out_shape=jax.ShapeDtypeStruct((2, NH, 2 * LANES), jnp.float32),
        scratch_shapes=[pltpu.VMEM((2, NF * NH, width), jnp.bfloat16)] * 2,
        compiler_params=pltpu.CompilerParams(vmem_limit_bytes=VMEM),
    )(rows, root)


def partners(value, axis, size, steps):
    return [lax.ppermute(value, axis, [(i, i ^ step) for i in range(size)]) for step in steps]


def finish_kernel(*refs):
    out_ref = refs[-1]
    summed = refs[0][...]
    for ref in refs[1:-1]:
        summed = summed + ref[...]
    weight_sum = summed[0, NB : NB + 1, NB : NB + 1]
    summed = summed * (1.0 / (16.0 * 0.375 * NFFT)) / weight_sum
    cut, turned = [], []
    for which in range(2):
        half = summed[:, :, which * LANES : (which + 1) * LANES]
        cut.append(jnp.stack([half[g][:, f * NH : (f + 1) * NH] for g in range(2) for f in range(NF // 2)]))
        turned.append(jnp.concatenate([half[g].T.reshape(NF // 2, NH, NH) for g in range(2)], axis=0))
    row = lax.broadcasted_iota(jnp.int32, (NF, NB, NB), 1)
    column = lax.broadcasted_iota(jnp.int32, (NF, NB, NB), 2)
    re_re = jnp.where(row <= column, cut[0][:, 0:NB, 0:NB], turned[0][:, 0:NB, 0:NB])
    im_im = jnp.where(row >= column, cut[0][:, 1:NH, 0:NB], turned[0][:, 0:NB, 1:NH])
    upper = jnp.concatenate([re_re, cut[1][:, 0:NB, 0:NB]], axis=2)
    lower = jnp.concatenate([turned[1][:, 0:NB, 0:NB], im_im], axis=2)
    out_ref[0:NB] = jnp.transpose(upper, (1, 0, 2))
    out_ref[NB:] = jnp.transpose(lower, (1, 0, 2))


def finish(terms):
    out = pl.pallas_call(
        finish_kernel,
        out_shape=jax.ShapeDtypeStruct((2 * NB, NF, 2 * NB), jnp.float32),
        compiler_params=pltpu.CompilerParams(vmem_limit_bytes=VMEM),
    )(*terms)
    return jnp.transpose(out, (1, 0, 2))


def sum_over(value, axis, size):
    rounds, step = [], 1
    while step < size:
        wide = step == 2 and 4 * step <= size
        rounds.append([c + (step > 1) for c in ([step, 2 * step, 3 * step] if wide else [step])])
        step *= 4 if wide else 2
    for steps in rounds[:-1]:
        value = sum(partners(value, axis, size, steps), value)
    return [value] + partners(value, axis, size, rounds[-1])


def make_local(n_space):
    def local(snapshots, weights):
        steps, components, points = snapshots.shape
        share = HALF // steps
        block = jnp.transpose(snapshots, (1, 0, 2))
        across = [[h * share + i for h in ORDER] for i in range(share)]
        if share > 1:
            block = block.reshape(components, steps, NH, share, -1)
            teams = [[h * share + i for i in range(share)] for h in range(NH)]
            block = lax.all_to_all(block, "space", split_axis=3, concat_axis=1, axis_index_groups=teams, tiled=True)
            block = block.reshape(components, HALF, -1)
        rows, root = transform(block, weights)
        rows = lax.all_to_all(rows, "space", split_axis=0, concat_axis=0, axis_index_groups=across, tiled=True)
        gram = local_gram(rows, root, n_space * steps)
        return finish(sum_over(gram, "space", n_space))

    return local


def solution(mesh):
    in_specs = (P(("grp", "space"), None, None), P(("grp", "space")))
    out_specs = P("grp", None, None)
    return jax.shard_map(
        make_local(mesh.shape["space"]), mesh=mesh, in_specs=in_specs, out_specs=out_specs, check_vma=False
    )
```

```python
import math

import numpy as np
import ml_dtypes
import jax
import jax.numpy as jnp
from jax import lax
from jax.experimental import pallas as pl
from jax.experimental.pallas import tpu as pltpu
from jax.sharding import PartitionSpec as P

NFFT = 128
NB = 15
NF = 16
HALF = NFFT // 2
NH = NB + 1
LANES = 128
ORDER = (11, 10, 7, 6, 15, 12, 3, 2, 14, 9, 0, 1, 5, 13, 4, 8)
MAIN = 2 * NF
EXTRA = 5
ROWS = 40
SMALLEST = 2.0**-60
SMALL_SUM = 256.0
LOWEST, STEEP = -125.0, 251.0
VMEM = 48 * 1024 * 1024


def half_table():
    turns = 2.0 * np.pi * np.arange(NF + 2)[:, None] * np.arange(HALF)[None, :] / NFFT
    re, im = np.cos(turns), -np.sin(turns)
    offset_re, offset_im = re.sum(1), im.sum(1)
    re0, im0 = re - re.mean(1, keepdims=True), im - im.mean(1, keepdims=True)
    table = np.zeros((ROWS, HALF))
    table[0:NF] = re0[1 : NF + 1]
    table[NF : 2 * NF] = im0[1 : NF + 1]
    table[32] = 1.0 / SMALL_SUM
    table[35] = re0[NF + 1]
    table[36] = im0[NF + 1]
    return table, (offset_re.tolist(), offset_im.tolist())


def pieces(table):
    high = table.astype(ml_dtypes.bfloat16)
    low = (table - high.astype(np.float64)).astype(ml_dtypes.bfloat16)
    for row in range(table.shape[0]):
        for _ in range(8):
            left = table[row].sum() - high[row].astype(np.float64).sum() - low[row].astype(np.float64).sum()
            moved = (low[row].astype(np.float64) + left).astype(ml_dtypes.bfloat16)
            error = np.abs(moved.astype(np.float64) - low[row].astype(np.float64) - left)
            at = int(np.argmin(error))
            if error[at] >= abs(left):
                break
            low[row, at] = moved[at]
    return np.concatenate([high, low], axis=1)


def spread(component):
    place = lax.broadcasted_iota(jnp.int32, (1, LANES), 1) + LANES * component
    turns = place.astype(jnp.float32) * 0.618034
    return 1.0 / (1.0 + 0.125 * (turns - jnp.floor(turns)))


def coded_of(values, sizes, scale):
    coded = jnp.exp2(sizes * (scale * STEEP) + LOWEST)
    return jnp.where(values < 0.0, -coded, coded)


def value_of(coded, scale):
    return (jnp.log2(jnp.abs(coded)) - LOWEST) * jnp.where(coded < 0.0, -scale, scale)


def transform_kernel(block_hbm, table_hbm, weight_hbm, out_ref, root_ref, block_ref, table_ref, weight_ref, sems):
    components, _, points = block_ref.shape
    copies = [pltpu.make_async_copy(block_hbm.at[c], block_ref.at[c], sems.at[c]) for c in range(components)]
    copies.append(pltpu.make_async_copy(table_hbm, table_ref, sems.at[components]))
    copies.append(pltpu.make_async_copy(weight_hbm, weight_ref, sems.at[components + 1]))
    for copy in copies:
        copy.start()
    for copy in copies:
        copy.wait()
    table = table_ref[...]
    place = lax.broadcasted_iota(jnp.int32, (8, 1), 0)
    place_of = [ORDER.index(h) for h in range(points // LANES)]
    many = math.gcd(points // LANES, 4)
    wide = many * LANES
    for p in range(points // wide):
        extras = []
        for c in range(components):
            block = block_ref[c, :, p * wide : (p + 1) * wide]
            rows = jnp.dot(table, jnp.concatenate([block] * 2, axis=0), preferred_element_type=jnp.float32)
            sizes = jnp.abs(rows)
            top = sizes[:, 0:LANES]
            for d in range(1, many):
                top = jnp.maximum(top, sizes[:, d * LANES : (d + 1) * LANES])
            halves = jnp.ceil(2.0 * jnp.log2(jnp.maximum(jnp.max(top, axis=0, keepdims=True), SMALLEST)))
            scale = jnp.exp2(halves * -0.5) * spread(c)
            scale, halves = (jnp.concatenate([x] * many, axis=1) for x in (scale, halves))
            whole = rows[32:33] * SMALL_SUM
            high = whole.astype(jnp.bfloat16).astype(jnp.float32)
            rows = jnp.concatenate([rows[0:32], jnp.where(place == 1, whole - high, rows[32:40])], axis=0)
            coded = coded_of(rows, jnp.abs(rows), scale)
            for d in range(many):
                out_ref[place_of[p * many + d], c * MAIN : (c + 1) * MAIN] = coded[0:MAIN, d * LANES : (d + 1) * LANES].astype(jnp.bfloat16)
            extras += [high, coded[33:34], coded[35:37], halves]
        extras.append(jnp.zeros((1, wide), jnp.float32))
        extras = jnp.concatenate(extras, axis=0).astype(jnp.bfloat16)
        for d in range(many):
            out_ref[place_of[p * many + d], components * MAIN :] = extras[:, d * LANES : (d + 1) * LANES]
    root_ref[...] = jnp.sqrt(weight_ref[...])


def gram_kernel(steps_all, offsets, rows_ref, root_ref, out_ref, high_ref, low_ref):
    components = (rows_ref.shape[1] - 1) // (MAIN + EXTRA)
    extra = components * MAIN
    group = NF // 2
    rows = jnp.stack([rows_ref[ORDER.index(h)] for h in range(NH)])
    rows = jnp.transpose(rows.astype(jnp.float32), (1, 0, 2))
    root = root_ref[...]
    last = lax.broadcasted_iota(jnp.int32, (NH, LANES), 0) == NB
    for c in range(components):
        further = rows[extra + c * EXTRA : extra + (c + 1) * EXTRA]
        scale = jnp.exp2(further[4] * 0.5) * (1.0 / (STEEP * spread(c)))
        sums = further[0] + value_of(further[1], scale)
        delta = (sums * (1.0 / HALF) - jnp.sum(sums, axis=0, keepdims=True) * (1.0 / steps_all)) * root
        scale = scale * root

        def value(i, k):
            coded = rows[c * MAIN + i * NF + k - 1] if k <= NF else further[2 + i]
            return value_of(coded, scale) + (offsets[i][k] * delta if k % 2 else 0.0)

        for i in range(2):
            before, here = (delta * float(HALF), jnp.zeros_like(delta))[i], value(i, 1)
            for k in range(1, NF + 1):
                after = value(i, k + 1)
                sides, twice = before + after, here + here
                back = pltpu.roll(twice + sides, NH - 1, 0)
                spectrum = twice - sides - back if k % 2 else twice - sides + back
                spectrum = jnp.where(last, root if i == 0 and c == 0 else 0.0, spectrum)
                high = spectrum.astype(jnp.bfloat16)
                g, f = (k - 1) // group, (k - 1) % group
                at = pl.ds((i * group + f) * NH, NH)
                high_ref[g, at, c * LANES : (c + 1) * LANES] = high
                low_ref[g, at, c * LANES : (c + 1) * LANES] = (spectrum - high.astype(jnp.float32)).astype(jnp.bfloat16)
                before, here = here, after
    row = lax.broadcasted_iota(jnp.int32, (NH, LANES), 0)
    column = lax.broadcasted_iota(jnp.int32, (NH, LANES), 1) % NH
    shared = lax.broadcasted_iota(jnp.int32, (NH, LANES), 1) // NH
    dims = (((1,), (1,)), ((), ()))
    for g in range(2):
        high, low = high_ref[g], low_ref[g]
        left, right = jnp.concatenate([high, high, low], 1), jnp.concatenate([high, low, high], 1)
        gram = lax.dot_general(left, right, dims, preferred_element_type=jnp.float32)
        gram = gram.reshape(2, group, NH, gram.shape[1])
        kept = []
        for i, j in ((0, 0), (1, 1), (0, 1)):
            block = jnp.zeros(shared.shape, jnp.float32)
            for f in range(group):
                block = block + jnp.where(shared == f, gram[i, f, :, j * LANES : (j + 1) * LANES], 0.0)
            kept.append(block)
        out_ref[g, :, 0:LANES] = jnp.where(column >= row, kept[0], jnp.concatenate([kept[0][0:1], kept[1][:-1]], 0))
        out_ref[g, :, LANES:] = kept[2]


def transform(block, weights):
    table, _ = half_table()
    components, _, points = block.shape
    table = pieces(table)
    return pl.pallas_call(
        transform_kernel,
        in_specs=[pl.BlockSpec(memory_space=pltpu.HBM)] * 3,
        out_shape=(
            jax.ShapeDtypeStruct((points // LANES, components * (MAIN + EXTRA) + 1, LANES), jnp.bfloat16),
            jax.ShapeDtypeStruct((1, LANES), jnp.float32),
        ),
        scratch_shapes=[
            pltpu.VMEM(block.shape, block.dtype),
            pltpu.VMEM(table.shape, jnp.bfloat16),
            pltpu.VMEM((1, LANES), jnp.float32),
            pltpu.SemaphoreType.DMA((components + 2,)),
        ],
        compiler_params=pltpu.CompilerParams(vmem_limit_bytes=VMEM),
    )(*[pltpu.with_memory_space_constraint(x, pltpu.HBM) for x in (block, jnp.asarray(table), weights[None, :])])


def local_gram(rows, root, steps_all):
    _, offsets = half_table()
    width = (rows.shape[1] - 1) // (MAIN + EXTRA) * LANES
    return pl.pallas_call(
        lambda *refs: gram_kernel(steps_all, offsets, *refs),
        out_shape=jax.ShapeDtypeStruct((2, NH, 2 * LANES), jnp.float32),
        scratch_shapes=[pltpu.VMEM((2, NF * NH, width), jnp.bfloat16)] * 2,
        compiler_params=pltpu.CompilerParams(vmem_limit_bytes=VMEM),
    )(rows, root)


def partners(value, axis, size, steps):
    return [lax.ppermute(value, axis, [(i, i ^ step) for i in range(size)]) for step in steps]


def finish_kernel(*refs):
    out_ref = refs[-1]
    summed = refs[0][...]
    for ref in refs[1:-1]:
        summed = summed + ref[...]
    weight_sum = summed[0, NB : NB + 1, NB : NB + 1]
    summed = summed * (1.0 / (16.0 * 0.375 * NFFT)) / weight_sum
    cut, turned = [], []
    for which in range(2):
        half = summed[:, :, which * LANES : (which + 1) * LANES]
        cut.append(jnp.stack([half[g][:, f * NH : (f + 1) * NH] for g in range(2) for f in range(NF // 2)]))
        turned.append(jnp.concatenate([half[g].T.reshape(NF // 2, NH, NH) for g in range(2)], axis=0))
    row = lax.broadcasted_iota(jnp.int32, (NF, NB, NB), 1)
    column = lax.broadcasted_iota(jnp.int32, (NF, NB, NB), 2)
    re_re = jnp.where(row <= column, cut[0][:, 0:NB, 0:NB], turned[0][:, 0:NB, 0:NB])
    im_im = jnp.where(row >= column, cut[0][:, 1:NH, 0:NB], turned[0][:, 0:NB, 1:NH])
    upper = jnp.concatenate([re_re, cut[1][:, 0:NB, 0:NB]], axis=2)
    lower = jnp.concatenate([turned[1][:, 0:NB, 0:NB], im_im], axis=2)
    out_ref[0:NB] = jnp.transpose(upper, (1, 0, 2))
    out_ref[NB:] = jnp.transpose(lower, (1, 0, 2))


def finish(terms):
    out = pl.pallas_call(
        finish_kernel,
        out_shape=jax.ShapeDtypeStruct((2 * NB, NF, 2 * NB), jnp.float32),
        compiler_params=pltpu.CompilerParams(vmem_limit_bytes=VMEM),
    )(*terms)
    return jnp.transpose(out, (1, 0, 2))


def sum_over(value, axis, size):
    rounds, step = [], 1
    while step < size:
        wide = step == 2 and 4 * step <= size
        rounds.append([c + (step > 1) for c in ([step, 2 * step, 3 * step] if wide else [step])])
        step *= 4 if wide else 2
    rounds.sort(key=len)
    for steps in rounds[:-1]:
        value = sum(partners(value, axis, size, steps), value)
    return [value] + partners(value, axis, size, rounds[-1])


def make_local(n_space):
    def local(snapshots, weights):
        steps, components, points = snapshots.shape
        share = HALF // steps
        block = jnp.transpose(snapshots, (1, 0, 2))
        across = [[h * share + i for h in ORDER] for i in range(share)]
        if share > 1:
            block = block.reshape(components, steps, NH, share, -1)
            teams = [[h * share + i for i in range(share)] for h in range(NH)]
            block = lax.all_to_all(block, "space", split_axis=3, concat_axis=1, axis_index_groups=teams, tiled=True)
            block = block.reshape(components, HALF, -1)
        rows, root = transform(block, weights)
        rows = lax.all_to_all(rows, "space", split_axis=0, concat_axis=0, axis_index_groups=across, tiled=True)
        gram = local_gram(rows, root, n_space * steps)
        return finish(sum_over(gram, "space", n_space))

    return local


def solution(mesh):
    in_specs = (P(("grp", "space"), None, None), P(("grp", "space")))
    out_specs = P("grp", None, None)
    return jax.shard_map(
        make_local(mesh.shape["space"]), mesh=mesh, in_specs=in_specs, out_specs=out_specs, check_vma=False
    )
```
